128 devices in a mesh: hst: 16 (over z, x), doc: 8 (over y, core).
Axes of the slice: x: 4, y: 4, z: 4, core: 2. Of those that a mesh axis runs over, the one named last changes fastest.
Arguments:
- docs: bfloat16 [1048576, 768], P(('hst', 'doc')), may hold values from -400 to 400, as said below
- w_in: bfloat16 [768, 256], replicated, may hold values from -0.21875 to 0.21875
- w_out: bfloat16 [256, 64], replicated, may hold values from -0.375 to 0.375
- doc_host: int32 [1048576], P(('hst', 'doc')), may hold values from 0 to 2047
- tiles: bfloat16 [8192, 128, 128], P(('hst', 'doc')), may hold values from 0 to 10, as said below
- dst_block: int32 [8192], P(('hst', 'doc')), may hold values from 0 to 15
- src_block: int32 [8192], P(('hst', 'doc')), may hold values from 0 to 255
- tile_count: int32 [128], P(('hst', 'doc')), may hold values from 1 to 64, as said below
- teleport: int32 [32768], P('hst'), may hold values 0 or 1
Outputs:
- scores: float32 [32768, 64], P(('hst', 'doc'))
The draws below stay inside these ranges and needn't reach their ends.
Inputs may be any that keep to these rules, and one draw needn't show every extreme that they name: `docs`: embeddings stay in the stated range. `tiles`: link weights are nonnegative. `tile_count`: some device uses all 64 slots.
All inputs are finite; a program needn't handle non-finite values. No bound on the sum of `teleport` on one device may be relied on, other than what follows from the above.
Results may differ from the reference program's by a relative error of at most 0.00066.
Values may be sent and summed in bfloat16 or wider, within the bound.
A program may use at most 128 MiB of HBM per device.

```python
import math
import jax
import jax.numpy as jnp
import numpy as np
from jax import lax

D = 768
HID = 256
TOPICS = 64
DOC_DEV = 8192
HOST_DEV = 2048
BLOCK = 128
TILE_DEV = 64
HOPS = 3
DOCS = 1048576
HOSTS = 32768
BLK_PART = 16
NBLK = 256
TILES = 8192
N_HST = 16
N_DOC = 8
DEVICES = 128


def draw_docs(key, part):
    first = jax.random.fold_in(key, 0)
    values = jnp.clip(jax.random.normal(first, (DOCS, D)), -5.0, 5.0)
    return values.astype(jnp.bfloat16)


def draw_tiles(key, part):
    value_key = jax.random.fold_in(key, 11)
    values = jax.random.uniform(value_key, (TILES, BLOCK, BLOCK), minval=0.0, maxval=1.0)
    low_end = 0.5
    high_end = 2.0
    exponent = 0.4
    row_level = jnp.exp(jax.random.uniform(jax.random.fold_in(key, 12), (TILES, BLOCK, 1), minval=jnp.log(low_end), maxval=jnp.log(high_end)))
    col_level = jnp.exp(jax.random.uniform(jax.random.fold_in(key, 13), (TILES, 1, BLOCK), minval=jnp.log(low_end), maxval=jnp.log(high_end)))
    chance = jnp.clip(row_level * col_level * 0.125, 0.0, 0.5)
    weight = jnp.maximum(values / chance, 0.01) ** (-exponent)
    weak_pick = jax.random.uniform(jax.random.fold_in(key, 14), (BLOCK,)) < 0.0625
    forced = jax.random.randint(jax.random.fold_in(key, 15), (), 0, BLOCK)
    weak_cols = jnp.logical_or(weak_pick, jnp.arange(BLOCK) == forced)
    damping = jnp.where(weak_cols, 0.001, 1.0)
    result_tiles = jnp.where(values < chance, weight, 0.0) * damping[None, None, :]
    return result_tiles.astype(jnp.bfloat16)


def draw_tile_count(key, part):
    counts = jax.random.randint(key, (DEVICES,), 1, TILE_DEV + 1)
    where = jax.random.randint(jax.random.fold_in(key, 1), (), 0, DEVICES)
    return counts.at[where].set(TILE_DEV).astype(jnp.int32)


def with_ends(result, rng, least, high):
    dims = result.shape
    spot = [jax.random.randint(jax.random.fold_in(rng, axis), (), 0, dims[axis]) for axis in range(len(dims))]
    result = result.at[tuple(spot)].set(least)
    longest = dims.index(max(dims))
    spot[longest] = (spot[longest] + 1) % dims[longest]
    return result.at[tuple(spot)].set(high)


def rank_table(number_of, lean):
    portions = [(1 << 20) // math.isqrt(grade ** lean) + 1 for grade in range(1, number_of + 1)]
    deviation = 1 + sum(portions) // (1 << 30)
    return np.cumsum(np.array([max(1, weight // deviation) for weight in portions]))


def ranked(own_key, dims, amount, slope):
    table = rank_table(amount, slope)
    lot = jax.random.randint(jax.random.fold_in(own_key, 1), dims, 0, int(table[amount - 1]))
    grade = jnp.searchsorted(jnp.asarray(table, jnp.int32), lot, side="right")
    return jax.random.permutation(jax.random.fold_in(own_key, 2), amount)[grade].astype(jnp.int32)


def scatter_about(rng, shape, width, limit, dtype=jnp.bfloat16):
    drawn = jax.random.normal(rng, shape, jnp.float32) * width
    return jnp.minimum(jnp.maximum(drawn, -limit), limit).astype(dtype)


def setup_inputs(seed: int = 0) -> dict:
    splits = jax.random.split(jax.random.key(seed), 10)
    docs = draw_docs(jax.random.fold_in(splits[9], 71), 0)
    w_in = scatter_about(splits[1], (D, HID), D ** -0.5, 0.21875)
    w_out = scatter_about(splits[2], (HID, TOPICS), HID ** -0.5, 0.375)
    doc_host = with_ends(ranked(splits[3], (DOCS,), HOST_DEV, 2), jax.random.fold_in(splits[3], 3), 0, HOST_DEV - 1).astype(jnp.int32)
    tiles = draw_tiles(jax.random.fold_in(splits[9], 71), 0)
    dst_block = with_ends(jax.random.randint(splits[5], (TILES,), 0, BLK_PART), jax.random.fold_in(splits[5], 1), 0, BLK_PART - 1).astype(jnp.int32)
    src_block = with_ends(jax.random.randint(splits[6], (TILES,), 0, NBLK), jax.random.fold_in(splits[6], 1), 0, NBLK - 1).astype(jnp.int32)
    tile_count = draw_tile_count(jax.random.fold_in(splits[9], 71), 0)
    teleport = with_ends((jax.random.randint(splits[8], (HOSTS,), 0, 4) < 1).astype(jnp.int32), jax.random.fold_in(splits[8], 1), 0, 1)
    return {"docs": docs, "w_in": w_in, "w_out": w_out, "doc_host": doc_host, "tiles": tiles, "dst_block": dst_block, "src_block": src_block, "tile_count": tile_count, "teleport": teleport}


def classify(block_docs, w_in, w_out):
    hidden = jax.nn.gelu(jnp.dot(block_docs, w_in, preferred_element_type=jnp.float32), approximate=True).astype(jnp.bfloat16)
    logits = jnp.dot(hidden, w_out, preferred_element_type=jnp.float32)
    return jax.nn.softmax(logits, axis=-1)


def reference(docs, w_in, w_out, doc_host, tiles, dst_block, src_block, tile_count, teleport):
    probs = lax.map(lambda b: classify(b, w_in, w_out), docs.reshape(DEVICES, DOC_DEV, D)).reshape(DOCS, TOPICS)
    doc_part = (jnp.arange(DOCS) // (DOC_DEV * N_DOC)).astype(jnp.int32)
    host_global = (doc_part * HOST_DEV + doc_host).astype(jnp.int32)
    host_topic = jax.ops.segment_sum(probs, host_global, num_segments=HOSTS)
    slot = jnp.arange(TILES)
    valid = ((slot % TILE_DEV) < tile_count[slot // TILE_DEV]).astype(jnp.float32)
    colsum = jnp.sum(tiles.astype(jnp.float32), axis=1) * valid[:, None]
    degree = jax.ops.segment_sum(colsum, src_block, num_segments=NBLK).reshape(HOSTS)
    inverse = 1.0 / jnp.maximum(degree, 1.0)
    member = teleport.astype(jnp.float32)[:, None]
    mass = jnp.sum(member * host_topic, axis=0)
    tele = member * host_topic / mass
    tiles_part = tiles.reshape(N_HST, TILE_DEV * N_DOC, BLOCK, BLOCK)
    dst_part = dst_block.reshape(N_HST, TILE_DEV * N_DOC)
    src_part = src_block.reshape(N_HST, TILE_DEV * N_DOC)
    valid_part = valid.reshape(N_HST, TILE_DEV * N_DOC)
    x = tele
    for hop in range(HOPS):
        sent = (x * inverse[:, None]).astype(jnp.bfloat16).reshape(NBLK, BLOCK, TOPICS)

        def part_flow(item):
            tile_set, dst, src, used = item
            slabs = sent[src].astype(jnp.float32)
            prod = jnp.einsum("kij,kjt->kit", tile_set.astype(jnp.float32), slabs, precision=lax.Precision.HIGHEST)
            prod = prod * used[:, None, None]
            return jax.ops.segment_sum(prod, dst, num_segments=BLK_PART)

        inflow = lax.map(part_flow, (tiles_part, dst_part, src_part, valid_part)).reshape(HOSTS, TOPICS)
        x = 0.85 * inflow + 0.15 * tele
    return HOSTS * x
```

```python
import functools
import jax
import jax.numpy as jnp
from jax import lax
from jax.experimental import pallas as pl
from jax.experimental.pallas import tpu as pltpu
from jax.sharding import PartitionSpec as P

HOPS = 3
MESH = pl.DeviceIdType.MESH
NT = (((1,), (1,)), ((), ()))


def local_kernel(
    dst_ref, src_ref, cnt_ref, docs_ref, win_ref, wout_ref, dh_ref, tiles_ref, tel_ref,
    lt_ref, stage_ref, meta_ref, acc_ref, colsum_ref,
):
    step = pl.program_id(0)
    steps = pl.num_programs(0)
    hosts = acc_ref.shape[0]
    topics = wout_ref.shape[1]
    slots = dst_ref.shape[0]
    nblk = lt_ref.shape[0]
    tiles_step = tiles_ref.shape[0]

    @pl.when(step == 0)
    def _():
        acc_ref[...] = jnp.zeros_like(acc_ref)
        stage_ref[...] = jnp.zeros_like(stage_ref)
        count = cnt_ref[0]

        def clear(i, carry):
            meta_ref[4, i] = 0
            return carry

        lax.fori_loop(0, nblk + 1, clear, 0)

        def tally(k, carry):
            key = jnp.where(k < count, dst_ref[k], nblk)
            meta_ref[4, key] = meta_ref[4, key] + 1
            return carry

        lax.fori_loop(0, slots, tally, 0)

        def spread(d, total):
            size = meta_ref[4, d]
            meta_ref[4, d] = total
            ends = total + size
            meta_ref[3, d] = jnp.maximum(ends - 1, 0)
            meta_ref[3, d + 32] = (size > 0).astype(jnp.int32)
            return ends

        lax.fori_loop(0, nblk + 1, spread, 0)

        def mark(k, carry):
            meta_ref[2, k] = 1
            return carry

        lax.fori_loop(0, slots, mark, 0)

        def first(d, carry):
            meta_ref[2, meta_ref[4, d]] = 0
            return carry

        lax.fori_loop(0, nblk + 1, first, 0)

        def place(k, carry):
            key = jnp.where(k < count, dst_ref[k], nblk)
            at = meta_ref[4, key]
            meta_ref[4, key] = at + 1
            meta_ref[0, at] = k
            meta_ref[1, at] = src_ref[k]
            return carry

        lax.fori_loop(0, slots, place, 0)

    hidden = jax.nn.gelu(
        jnp.dot(docs_ref[...], win_ref[...], preferred_element_type=jnp.float32), approximate=True
    ).astype(jnp.bfloat16)
    logits = jnp.dot(hidden, wout_ref[...], preferred_element_type=jnp.float32)
    weight = jnp.exp(logits - jnp.max(logits, axis=-1, keepdims=True))
    probs = weight / jnp.sum(weight, axis=-1, keepdims=True)
    high = probs.astype(jnp.bfloat16)
    low = (probs - high.astype(jnp.float32)).astype(jnp.bfloat16)
    both = jnp.concatenate([high, low], axis=1)
    owner = dh_ref[0]
    piece = 256
    for at in range(0, hosts, piece):
        row = lax.broadcasted_iota(jnp.int32, (piece, owner.shape[1]), 0) + at
        onehot = jnp.where(row == owner, 1.0, 0.0).astype(jnp.bfloat16)
        acc_ref[at : at + piece] += jnp.dot(onehot, both, preferred_element_type=jnp.float32)

    colsum_ref[...] = jnp.sum(tiles_ref[...].astype(jnp.float32), axis=1)
    for i in range(tiles_step):
        k = step * tiles_step + i
        used = jnp.where(k < cnt_ref[0], 1.0, 0.0)
        b = src_ref[k]
        row = (b // 4) * 8 + b % 4
        stage_ref[pl.ds(row, 1), :] += colsum_ref[i : i + 1, :] * used

    @pl.when(step == steps - 1)
    def _():
        mass = jnp.zeros((topics, 128), jnp.float32)
        for b in range(nblk):
            block = acc_ref[b * 128 : (b + 1) * 128]
            flat = jnp.transpose(block)
            flat = flat[:topics] + flat[topics:]
            lt_ref[b] = flat
            mass += flat * tel_ref[b : b + 1, :].astype(jnp.float32)
        wide = jnp.concatenate([mass, jnp.zeros_like(mass)], axis=0)
        mass_row = jnp.sum(jnp.transpose(wide), axis=0, keepdims=True)
        for j in range(stage_ref.shape[0] // 8):
            stage_ref[j * 8 + 4 : j * 8 + 5, :] = mass_row


def peer(dz, dx, dy, dc):
    h, d = lax.axis_index("hst"), lax.axis_index("doc")
    z = lax.rem(h // 4 + dz, 4)
    x = lax.rem(lax.rem(h, 4) + dx, 4)
    y = lax.rem(d // 2 + dy, 4)
    c = lax.rem(lax.rem(d, 2) + dc, 2)
    return (z * 4 + x, y * 2 + c)


PLANE = [(z, x, 0, 0) for z in range(4) for x in range(4) if z or x]
GROUP = [(0, 0, y, c) for y in range(4) for c in range(2) if y or c]
SIBLING = (0, 0, 0, 1)
ORDERS = (("x", "z", "y", 0, 3), ("z", "y", "x", 3, 3), ("y", "x", "z", 6, 2))


def net_kernel(
    meta_ref, lt_ref, stage_ref, meta_any, tiles_any, tel_ref, out_ref,
    own_tiles, sib_tiles, sib_meta, sib_smem, lt_in, stage_in, group_sum, group_in, part, rs_in,
    tele, state, all0, all1, all2, runs, final,
    loc_sem, sib_send, sib_recv, st_send, st_recv, gr_send, gr_recv, rs_send, rs_recv, ag_send, ag_recv,
):
    h, d = lax.axis_index("hst"), lax.axis_index("doc")
    pos = {"z": h // 4, "x": lax.rem(h, 4), "y": d // 2}
    core = lax.rem(d, 2)
    y = pos["y"]

    def remote(src, dst, send, recv, to):
        return pltpu.make_async_remote_copy(
            src_ref=src, dst_ref=dst, send_sem=send, recv_sem=recv, device_id=peer(*to), device_id_type=MESH
        )

    barrier = pltpu.get_barrier_semaphore()
    for to in PLANE + GROUP:
        pl.semaphore_signal(barrier, inc=1, device_id=peer(*to), device_id_type=MESH)
    pl.semaphore_wait(barrier, len(PLANE) + len(GROUP))

    mine = pl.multiple_of(core * 32, 32)
    other = pl.multiple_of(32 - core * 32, 32)
    lt_copy = remote(lt_ref.at[:, pl.ds(other, 32), :], lt_in, sib_send.at[0], sib_recv.at[0], SIBLING)
    lt_copy.start()
    stage_copies = []
    for j, to in enumerate(PLANE):
        there = peer(*to)[0]
        stage_copies.append(remote(stage_ref.at[there], stage_in.at[j], st_send.at[j], st_recv.at[j], to))
    for copy in stage_copies:
        copy.start()
    meta_copy = remote(meta_any, sib_meta, sib_send.at[1], sib_recv.at[1], SIBLING)
    meta_copy.start()
    tile_copy = remote(tiles_any, sib_tiles, sib_send.at[2], sib_recv.at[2], SIBLING)
    tile_copy.start()
    own_copy = pltpu.make_async_copy(tiles_any, own_tiles, loc_sem.at[0])
    own_copy.start()

    def reduce_start(inst):
        copies = []
        for k in range(1, 4):
            there = lax.rem(y + k, 4)
            copies.append(
                remote(
                    part.at[pl.ds(there * 4, 4)], rs_in.at[inst, k - 1],
                    rs_send.at[inst, k - 1], rs_recv.at[inst, k - 1], (0, 0, k, 0),
                )
            )
        for copy in copies:
            copy.start()
        return copies

    def reduce_end(inst, copies):
        for copy in copies:
            copy.wait_recv()
        total = part[pl.ds(y * 4, 4)] + rs_in[inst, 0] + rs_in[inst, 1] + rs_in[inst, 2]
        for copy in copies:
            copy.wait_send()
        return total

    lt_copy.wait()
    part[...] = lt_ref[:, pl.ds(mine, 32), :] + lt_in[...]
    copies = reduce_start(0)

    for copy in stage_copies:
        copy.wait_recv()
    total = stage_ref[h]
    for j in range(len(PLANE)):
        total += stage_in[j]
    group_sum[...] = total
    group_copies = []
    for j, to in enumerate(GROUP):
        there = peer(*to)[1] // 2
        group_copies.append(remote(group_sum.at[there], group_in.at[j], gr_send.at[j], gr_recv.at[j], to))
    for copy in group_copies:
        copy.start()
    for copy in stage_copies:
        copy.wait_send()
    meta_copy.wait()
    meta_local = pltpu.make_async_copy(sib_meta, sib_smem, loc_sem.at[1])
    meta_local.start()

    topic = reduce_end(0, copies)
    for copy in group_copies:
        copy.wait_recv()
    total = group_sum[y]
    for j in range(len(GROUP)):
        total += group_in[j]
    for copy in group_copies:
        copy.wait_send()
    inverse = (1.0 / jnp.maximum(total[0:4], 1.0))[:, None, :]
    square = jnp.transpose(jnp.broadcast_to(total[4:5], (128, 128)))
    mass = jnp.where(core == 0, square[0:32], square[32:64])
    member = tel_ref[pl.ds(y * 4, 4), :].astype(jnp.float32)[:, None, :]
    start = member * topic / mass[None]
    tele[...] = start
    state[...] = start
    meta_local.wait()
    own_copy.wait()
    tile_copy.wait()

    def hop_body(hop, gathered):
        def place(fixed, first, count):
            index = [fixed[axis] if axis in fixed else slice(None) for axis in "zxy"]
            return gathered.at[(*index, pl.ds(first, count))]

        sent = (state[...] * inverse).astype(jnp.bfloat16)
        gathered[pos["z"], pos["x"], y] = sent.reshape(8, 16, 128)
        started = []

        def along(axis, k):
            return tuple(k if axis == name else 0 for name in "zxy") + (0,)

        def send(o, slot, axis, k, ref):
            copy = remote(ref, ref, ag_send.at[hop, o, slot], ag_recv.at[hop, o, slot], along(axis, k))
            copy.start()
            started.append(copy)
            return copy

        one = []
        for o, (a1, a2, a3, first, count) in enumerate(ORDERS):
            ref = place(pos, first, count)
            one.append([send(o, k - 1, a1, k, ref) for k in range(1, 4)])
        two, three = [], []
        for o, (a1, a2, a3, first, count) in enumerate(ORDERS):
            for copy in one[o]:
                copy.wait_recv()
            ref = place({a2: pos[a2], a3: pos[a3]}, first, count)
            two.append([send(o, 2 + k, a2, k, ref) for k in range(1, 4)])
            three += [send(o, 5 + k, a3, k, ref) for k in range(1, 4)]
        for k2 in range(1, 4):
            for o, (a1, a2, a3, first, count) in enumerate(ORDERS):
                two[o][k2 - 1].wait_recv()
                there = lax.rem(pos[a2] + 4 - k2, 4)
                ref = place({a2: there, a3: pos[a3]}, first, count)
                three += [send(o, 5 + 3 * k2 + k, a3, k, ref) for k in range(1, 4)]
        for copy in three:
            copy.wait_recv()

        lists = ((meta_ref, own_tiles), (sib_smem, sib_tiles))
        batch = 8

        def tile_body(i, run):
            run = list(run)
            for j in range(batch):
                r = i * batch + j
                for n, (m, t) in enumerate(lists):
                    b = m[1, r]
                    slab = gathered[b // 64, (b // 16) % 4, (b // 4) % 4, pl.ds((b % 4) * 2, 2)]
                    prod = lax.dot_general(
                        slab.reshape(32, 128), t[m[0, r]], NT, preferred_element_type=jnp.float32
                    )
                    run[n] = jnp.where(m[2, r] > 0, run[n], 0.0) + prod
                    runs[n, r] = run[n]
            return tuple(run)

        zero = jnp.zeros((32, 128), jnp.float32)
        lax.fori_loop(0, own_tiles.shape[0] // batch, tile_body, (zero, zero))
        for blk in range(16):
            value = zero
            for n, (m, t) in enumerate(lists):
                value += jnp.where(m[3, blk + 32] > 0, runs[n, m[3, blk]], 0.0)
            part[blk] = value
        inflow = reduce_end(hop + 1, reduce_start(hop + 1))
        state[...] = 0.85 * inflow + 0.15 * tele[...]
        for copy in started:
            copy.wait_send()

    for hop, gathered in enumerate((all0, all1, all2)):
        hop_body(hop, gathered)

    hosts_all = 128.0 * 256.0
    keep = pl.multiple_of(core * 2, 2)
    give = pl.multiple_of(2 - core * 2, 2)
    state[...] = hosts_all * state[...]
    last = remote(
        state.at[pl.ds(give, 2)], final.at[:, pl.ds(mine, 32), :], sib_send.at[3], sib_recv.at[3], SIBLING
    )
    last.start()
    final[:, pl.ds(mine, 32), :] = state[pl.ds(keep, 2)]
    last.wait()
    for j in range(2):
        out_ref[j * 128 : (j + 1) * 128, :] = jnp.transpose(final[j])


def body(docs, w_in, w_out, doc_host, tiles, dst_block, src_block, tile_count, teleport):
    f32, bf16, i32 = jnp.float32, jnp.bfloat16, jnp.int32
    docs_dev, depth = docs.shape
    hidden, topics = w_out.shape
    slots = tiles.shape[0]
    hosts = teleport.shape[0]
    steps = 8
    rows = docs_dev // steps
    smem = pl.BlockSpec(memory_space=pltpu.SMEM)
    vmem = pl.BlockSpec(memory_space=pltpu.VMEM)
    anyw = pl.BlockSpec(memory_space=pl.ANY)
    member = teleport.reshape(16, 128)
    local_topic, stage, meta = pl.pallas_call(
        local_kernel,
        grid=(steps,),
        out_shape=(
            jax.ShapeDtypeStruct((16, topics, 128), f32),
            jax.ShapeDtypeStruct((512, 128), f32),
            jax.ShapeDtypeStruct((8, 128), i32),
        ),
        in_specs=[
            smem, smem, smem,
            pl.BlockSpec((rows, depth), lambda i: (i, 0)),
            pl.BlockSpec((depth, hidden), lambda i: (0, 0)),
            pl.BlockSpec((hidden, topics), lambda i: (0, 0)),
            pl.BlockSpec((1, 1, rows), lambda i: (i, 0, 0)),
            pl.BlockSpec((slots // steps, 128, 128), lambda i: (i, 0, 0)),
            pl.BlockSpec((16, 128), lambda i: (0, 0)),
        ],
        out_specs=(
            pl.BlockSpec((16, topics, 128), lambda i: (0, 0, 0)),
            pl.BlockSpec((512, 128), lambda i: (0, 0)),
            smem,
        ),
        scratch_shapes=[pltpu.VMEM((hosts, 128), f32), pltpu.VMEM((slots // steps, 128), f32)],
        compiler_params=pltpu.CompilerParams(vmem_limit_bytes=56 << 20),
        name="classify",
    )(
        dst_block, src_block, tile_count, docs, w_in, w_out,
        doc_host.reshape(steps, 1, rows), tiles, member,
    )
    dma = pltpu.SemaphoreType.DMA
    return pl.pallas_call(
        net_kernel,
        out_shape=jax.ShapeDtypeStruct((256, topics), f32),
        in_specs=[smem, vmem, vmem, anyw, anyw, vmem],
        out_specs=vmem,
        scratch_shapes=[
            pltpu.VMEM(tiles.shape, bf16),
            pltpu.VMEM(tiles.shape, bf16),
            pltpu.VMEM((8, 128), i32),
            pltpu.SMEM((8, 128), i32),
            pltpu.VMEM((16, 32, 128), f32),
            pltpu.VMEM((15, 4, 8, 128), f32),
            pltpu.VMEM((4, 8, 128), f32),
            pltpu.VMEM((7, 8, 128), f32),
            pltpu.VMEM((16, 32, 128), f32),
            pltpu.VMEM((HOPS + 1, 3, 4, 32, 128), f32),
            pltpu.VMEM((4, 32, 128), f32),
            pltpu.VMEM((4, 32, 128), f32),
            pltpu.VMEM((4, 4, 4, 8, 16, 128), bf16),
            pltpu.VMEM((4, 4, 4, 8, 16, 128), bf16),
            pltpu.VMEM((4, 4, 4, 8, 16, 128), bf16),
            pltpu.VMEM((2, slots, 32, 128), f32),
            pltpu.VMEM((2, 64, 128), f32),
            dma((2,)), dma((4,)), dma((4,)), dma((15,)), dma((15,)), dma((7,)), dma((7,)),
            dma((HOPS + 1, 3)), dma((HOPS + 1, 3)), dma((HOPS, 3, 18)), dma((HOPS, 3, 18)),
        ],
        compiler_params=pltpu.CompilerParams(
            collective_id=0, has_side_effects=True, vmem_limit_bytes=56 << 20
        ),
        name="spread",
    )(meta, local_topic, stage.reshape(16, 4, 8, 128), meta, tiles, member)


def solution(mesh):
    placed = (
        P(("hst", "doc"), None),
        P(),
        P(),
        P(("hst", "doc")),
        P(("hst", "doc"), None, None),
        P(("hst", "doc")),
        P(("hst", "doc")),
        P(("hst", "doc")),
        P("hst"),
    )
    return jax.shard_map(
        body, mesh=mesh, in_specs=placed, out_specs=P(("hst", "doc"), None), check_vma=False
    )
```

```python
import functools
import jax
import jax.numpy as jnp
from jax import lax
from jax.experimental import pallas as pl
from jax.experimental.pallas import tpu as pltpu
from jax.sharding import PartitionSpec as P

HOPS = 3
MESH = pl.DeviceIdType.MESH
NT = (((1,), (1,)), ((), ()))


def local_kernel(
    dst_ref, src_ref, cnt_ref, docs_ref, win_ref, wout_ref, dh_ref, tiles_ref, tel_ref,
    lt_ref, stage_ref, meta_ref, acc_ref, colsum_ref,
):
    step = pl.program_id(0)
    steps = pl.num_programs(0)
    topics = wout_ref.shape[0]
    slots = dst_ref.shape[0]
    nblk = lt_ref.shape[0]
    tiles_step = tiles_ref.shape[0]

    @pl.when(step == 0)
    def _():
        acc_ref[...] = jnp.zeros_like(acc_ref)
        stage_ref[...] = jnp.zeros_like(stage_ref)
        count = cnt_ref[0]

        def clear(i, carry):
            meta_ref[4, i] = 0
            return carry

        lax.fori_loop(0, nblk + 1, clear, 0)

        def tally(k, carry):
            key = jnp.where(k < count, dst_ref[k], nblk)
            meta_ref[4, key] = meta_ref[4, key] + 1
            return carry

        lax.fori_loop(0, slots, tally, 0)

        def spread(d, total):
            size = meta_ref[4, d]
            meta_ref[4, d] = total
            ends = total + size
            meta_ref[3, d] = jnp.maximum(ends - 1, 0)
            meta_ref[3, d + 32] = (size > 0).astype(jnp.int32)
            return ends

        lax.fori_loop(0, nblk + 1, spread, 0)

        def mark(k, carry):
            meta_ref[2, k] = 1
            return carry

        lax.fori_loop(0, slots, mark, 0)

        def first(d, carry):
            meta_ref[2, meta_ref[4, d]] = 0
            return carry

        lax.fori_loop(0, nblk + 1, first, 0)

        def place(k, carry):
            key = jnp.where(k < count, dst_ref[k], nblk)
            at = meta_ref[4, key]
            meta_ref[4, key] = at + 1
            meta_ref[0, at] = k
            meta_ref[1, at] = src_ref[k]
            return carry

        lax.fori_loop(0, slots, place, 0)


    owner = dh_ref[0]
    upper = jnp.where(owner >= 1024, 1.0, 0.0).astype(jnp.bfloat16)
    lower = jnp.where(owner >= 1024, 0.0, 1.0).astype(jnp.bfloat16)
    pts = []
    for c in range(0, docs_ref.shape[0], 1024):
        hidden = jax.nn.gelu(
            jnp.dot(docs_ref[c:c+1024], win_ref[...], preferred_element_type=jnp.float32), approximate=True
        ).astype(jnp.bfloat16)
        logits = lax.dot_general(wout_ref[...], hidden, NT, preferred_element_type=jnp.float32)
        weight = jnp.exp(logits - jnp.max(logits, axis=0, keepdims=True))
        probs = weight / jnp.sum(weight, axis=0, keepdims=True)
        high = probs.astype(jnp.bfloat16)
        low = (probs - high.astype(jnp.float32)).astype(jnp.bfloat16)
        both = jnp.concatenate([high, low], axis=0)
        pts.append(jnp.concatenate([both * lower[:, c:c+1024], both * upper[:, c:c+1024]], axis=0))
    pt = jnp.concatenate(pts, axis=1)
    spot = (owner & 1023)
    piece = 512
    for at in range(0, 1024, piece):
        row = (lax.broadcasted_iota(jnp.int32, (piece, owner.shape[1]), 0) + at)
        onehot = jnp.where(row == spot, 1.0, 0.0).astype(jnp.bfloat16)
        acc_ref[at : at + piece] += lax.dot_general(onehot, pt, NT, preferred_element_type=jnp.float32)
    colsum_ref[...] = jnp.sum(tiles_ref[...].astype(jnp.float32), axis=1)
    for i in range(tiles_step):
        k = step * tiles_step + i
        used = jnp.where(k < cnt_ref[0], 1.0, 0.0)
        b = src_ref[k]
        row = (b // 4) * 8 + b % 4
        stage_ref[pl.ds(row, 1), :] += colsum_ref[i : i + 1, :] * used

    @pl.when(step == steps - 1)
    def _():
        mass = jnp.zeros((topics, 128), jnp.float32)
        for b in range(nblk):
            block = acc_ref[b % 8 * 128 : (b % 8 + 1) * 128, b // 8 * 128 : (b // 8 + 1) * 128]
            flat = jnp.transpose(block)
            flat = flat[:topics] + flat[topics:]
            lt_ref[b] = flat
            mass += flat * tel_ref[b : b + 1, :].astype(jnp.float32)
        wide = jnp.concatenate([mass, jnp.zeros_like(mass)], axis=0)
        mass_row = jnp.sum(jnp.transpose(wide), axis=0, keepdims=True)
        for j in range(stage_ref.shape[0] // 8):
            stage_ref[j * 8 + 4 : j * 8 + 5, :] = mass_row


def peer(dz, dx, dy, dc):
    h, d = lax.axis_index("hst"), lax.axis_index("doc")
    z = lax.rem(h // 4 + dz, 4)
    x = lax.rem(lax.rem(h, 4) + dx, 4)
    y = lax.rem(d // 2 + dy, 4)
    c = lax.rem(lax.rem(d, 2) + dc, 2)
    return (z * 4 + x, y * 2 + c)


PLANE = [(z, x, 0, 0) for z in range(4) for x in range(4) if z or x]
GROUP = [(0, 0, y, c) for y in range(4) for c in range(2) if y or c]
SIBLING = (0, 0, 0, 1)
STREAMS = 2
ORDERS = (
    (("x", "z", "y", 0, 1), ("z", "y", "x", 1, 2), ("y", "x", "z", 3, 1)),
    (("x", "z", "y", 0, 1), ("z", "y", "x", 1, 1), ("y", "x", "z", 2, 2)),
)


def net_kernel(
    meta_ref, lt_ref, stage_ref, meta_any, tiles_any, tel_ref, out_ref,
    own_tiles, sib_tiles, sib_meta, sib_smem, lt_in, stage_in, group_sum, group_in, part, rs_in,
    tele, state, g00, g01, g10, g11, g20, g21, runs, final,
    loc_sem, sib_send, sib_recv, st_send, st_recv, gr_send, gr_recv, rs_send, rs_recv, ag_send, ag_recv,
):
    h, d = lax.axis_index("hst"), lax.axis_index("doc")
    pos = {"z": h // 4, "x": lax.rem(h, 4), "y": d // 2}
    core = lax.rem(d, 2)
    y = pos["y"]

    def remote(src, dst, send, recv, to):
        return pltpu.make_async_remote_copy(
            src_ref=src, dst_ref=dst, send_sem=send, recv_sem=recv, device_id=peer(*to), device_id_type=MESH
        )

    barrier = pltpu.get_barrier_semaphore()
    for to in PLANE + GROUP:
        pl.semaphore_signal(barrier, inc=1, device_id=peer(*to), device_id_type=MESH)
    pl.semaphore_wait(barrier, len(PLANE) + len(GROUP))

    mine = pl.multiple_of(core * 32, 32)
    other = pl.multiple_of(32 - core * 32, 32)
    lt_copy = remote(lt_ref.at[:, pl.ds(other, 32), :], lt_in, sib_send.at[0], sib_recv.at[0], SIBLING)
    lt_copy.start()
    stage_copies = []
    for j, to in enumerate(PLANE):
        there = peer(*to)[0]
        stage_copies.append(remote(stage_ref.at[there], stage_in.at[j], st_send.at[j], st_recv.at[j], to))
    for copy in stage_copies:
        copy.start()
    meta_copy = remote(meta_any, sib_meta, sib_send.at[1], sib_recv.at[1], SIBLING)
    meta_copy.start()
    tile_copy = remote(tiles_any, sib_tiles, sib_send.at[2], sib_recv.at[2], SIBLING)
    tile_copy.start()
    own_copy = pltpu.make_async_copy(tiles_any, own_tiles, loc_sem.at[0])
    own_copy.start()

    def reduce_start(inst, s):
        copies = []
        for k in range(1, 4):
            there = lax.rem(y + k, 4)
            copies.append(
                remote(
                    part.at[s, pl.ds(there * 4, 4)], rs_in.at[inst, s, k - 1],
                    rs_send.at[inst, s, k - 1], rs_recv.at[inst, s, k - 1], (0, 0, k, 0),
                )
            )
        for copy in copies:
            copy.start()
        return copies

    def reduce_end(inst, s, copies):
        for copy in copies:
            copy.wait_recv()
        total = part[s, pl.ds(y * 4, 4)] + rs_in[inst, s, 0] + rs_in[inst, s, 1] + rs_in[inst, s, 2]
        for copy in copies:
            copy.wait_send()
        return total

    lt_copy.wait()
    whole = lt_ref[:, pl.ds(mine, 32), :] + lt_in[...]
    copies = []
    for s in range(STREAMS):
        part[s] = whole[:, s * 16 : s * 16 + 16]
        copies.append(reduce_start(0, s))

    for copy in stage_copies:
        copy.wait_recv()
    total = stage_ref[h]
    for j in range(len(PLANE)):
        total += stage_in[j]
    group_sum[...] = total
    group_copies = []
    for j, to in enumerate(GROUP):
        there = peer(*to)[1] // 2
        group_copies.append(remote(group_sum.at[there], group_in.at[j], gr_send.at[j], gr_recv.at[j], to))
    for copy in group_copies:
        copy.start()
    for copy in stage_copies:
        copy.wait_send()
    meta_copy.wait()
    meta_local = pltpu.make_async_copy(sib_meta, sib_smem, loc_sem.at[1])
    meta_local.start()

    topic = [reduce_end(0, s, copies[s]) for s in range(STREAMS)]
    for copy in group_copies:
        copy.wait_recv()
    total = group_sum[y]
    for j in range(len(GROUP)):
        total += group_in[j]
    for copy in group_copies:
        copy.wait_send()
    inverse = (1.0 / jnp.maximum(total[0:4], 1.0))[:, None, :]
    square = jnp.transpose(jnp.broadcast_to(total[4:5], (128, 128)))
    mass = jnp.where(core == 0, square[0:32], square[32:64])
    member = tel_ref[pl.ds(y * 4, 4), :].astype(jnp.float32)[:, None, :]
    for s in range(STREAMS):
        start = member * topic[s] / mass[None, s * 16 : s * 16 + 16]
        tele[s] = start
        state[s] = start
    meta_local.wait()
    own_copy.wait()
    tile_copy.wait()

    def along(axis, k):
        return tuple(k if axis == name else 0 for name in "zxy") + (0,)

    class Stream:
        def __init__(self, hop, s, gathered):
            self.hop, self.s, self.gathered, self.started = hop, s, gathered, []

        def place(self, fixed, first, count):
            index = [fixed[axis] if axis in fixed else slice(None) for axis in "zxy"]
            return self.gathered.at[(*index, pl.ds(first, count))]

        def send(self, o, slot, axis, k, ref):
            at = (self.hop, self.s, o, slot)
            copy = remote(ref, ref, ag_send.at[at], ag_recv.at[at], along(axis, k))
            copy.start()
            self.started.append(copy)
            return copy

        def stage1(self):
            sent = (state[self.s] * inverse).astype(jnp.bfloat16)
            self.gathered[pos["z"], pos["x"], y] = sent
            self.one = []
            for o, (a1, a2, a3, first, count) in enumerate(ORDERS[self.s]):
                ref = self.place(pos, first, count)
                self.one.append([self.send(o, k - 1, a1, k, ref) for k in range(1, 4)])

        def stage2(self):
            self.two, self.three = [], []
            for o, (a1, a2, a3, first, count) in enumerate(ORDERS[self.s]):
                for copy in self.one[o]:
                    copy.wait_recv()
                ref = self.place({a2: pos[a2], a3: pos[a3]}, first, count)
                self.two.append([self.send(o, 2 + k, a2, k, ref) for k in range(1, 4)])
                self.three += [self.send(o, 5 + k, a3, k, ref) for k in range(1, 4)]

        def stage3(self):
            for k2 in (1, 3, 2):
                for o, (a1, a2, a3, first, count) in enumerate(ORDERS[self.s]):
                    self.two[o][k2 - 1].wait_recv()
                    there = lax.rem(pos[a2] + 4 - k2, 4)
                    ref = self.place({a2: there, a3: pos[a3]}, first, count)
                    self.three += [self.send(o, 5 + 3 * k2 + k, a3, k, ref) for k in range(1, 4)]

        def multiply(self):
            for copy in self.three:
                copy.wait_recv()
            lists = ((meta_ref, own_tiles), (sib_smem, sib_tiles))
            batch = 32
            gathered, s = self.gathered, self.s

            def tile_body(i, run):
                run = list(run)
                for j in range(batch):
                    r = i * batch + j
                    for n, (m, t) in enumerate(lists):
                        b = m[1, r]
                        slab = gathered[b // 64, (b // 16) % 4, (b // 4) % 4, b % 4]
                        prod = lax.dot_general(slab, t[m[0, r]], NT, preferred_element_type=jnp.float32)
                        run[n] = jnp.where(m[2, r] > 0, run[n], 0.0) + prod
                        runs[n, r] = run[n]
                return tuple(run)

            zero = jnp.zeros((16, 128), jnp.float32)
            lax.fori_loop(0, own_tiles.shape[0] // batch, tile_body, (zero, zero))
            for blk in range(16):
                value = zero
                for n, (m, t) in enumerate(lists):
                    value += jnp.where(m[3, blk + 32] > 0, runs[n, m[3, blk]], 0.0)
                part[s, blk] = value
            self.reducing = reduce_start(self.hop + 1, s)

        def finish(self):
            inflow = reduce_end(self.hop + 1, self.s, self.reducing)
            state[self.s] = 0.85 * inflow + 0.15 * tele[self.s]

        def settle(self):
            for copy in self.started:
                copy.wait_send()

    streams = [[Stream(hop, s, g) for s, g in enumerate(gs)] for hop, gs in enumerate(((g00, g01), (g10, g11), (g20, g21)))]
    for one in streams[0]:
        one.stage1()
    for hop in range(HOPS):
        for one in streams[hop]:
            one.stage2()
        for one in streams[hop]:
            one.stage3()
        for one in streams[hop]:
            one.multiply()
        for s, one in enumerate(streams[hop]):
            one.finish()
            if hop + 1 < HOPS:
                streams[hop + 1][s].stage1()
        for one in streams[hop]:
            one.settle()

    hosts_all = 128.0 * 256.0
    keep = pl.multiple_of(core * 2, 2)
    give = pl.multiple_of(2 - core * 2, 2)
    state[...] = hosts_all * state[...]
    last = remote(state.at[:, pl.ds(give, 2)], final.at[core], sib_send.at[3], sib_recv.at[3], SIBLING)
    last.start()
    final[core] = state[:, pl.ds(keep, 2)]
    last.wait()
    for j in range(2):
        out_ref[j * 128 : (j + 1) * 128, :] = jnp.transpose(final[:, :, j].reshape(64, 128))


def body(docs, w_in, w_out, doc_host, tiles, dst_block, src_block, tile_count, teleport):
    f32, bf16, i32 = jnp.float32, jnp.bfloat16, jnp.int32
    docs_dev, depth = docs.shape
    hidden, topics = w_out.shape
    slots = tiles.shape[0]
    hosts = teleport.shape[0]
    steps = 8
    rows = docs_dev // steps
    smem = pl.BlockSpec(memory_space=pltpu.SMEM)
    vmem = pl.BlockSpec(memory_space=pltpu.VMEM)
    anyw = pl.BlockSpec(memory_space=pl.ANY)
    member = teleport.reshape(16, 128)
    local_topic, stage, meta = pl.pallas_call(
        local_kernel,
        grid=(steps,),
        out_shape=(
            jax.ShapeDtypeStruct((16, topics, 128), f32),
            jax.ShapeDtypeStruct((512, 128), f32),
            jax.ShapeDtypeStruct((8, 128), i32),
        ),
        in_specs=[
            smem, smem, smem,
            pl.BlockSpec((rows, depth), lambda i: (i, 0)),
            pl.BlockSpec((depth, hidden), lambda i: (0, 0)),
            pl.BlockSpec((topics, hidden), lambda i: (0, 0)),
            pl.BlockSpec((1, 1, rows), lambda i: (i, 0, 0)),
            pl.BlockSpec((slots // steps, 128, 128), lambda i: (i, 0, 0)),
            pl.BlockSpec((16, 128), lambda i: (0, 0)),
        ],
        out_specs=(
            pl.BlockSpec((16, topics, 128), lambda i: (0, 0, 0)),
            pl.BlockSpec((512, 128), lambda i: (0, 0)),
            smem,
        ),
        scratch_shapes=[pltpu.VMEM((1024, 256), f32), pltpu.VMEM((slots // steps, 128), f32)],
        compiler_params=pltpu.CompilerParams(vmem_limit_bytes=56 << 20),
        name="classify",
    )(
        dst_block, src_block, tile_count, docs, w_in, w_out.T,
        doc_host.reshape(steps, 1, rows), tiles, member,
    )
    dma = pltpu.SemaphoreType.DMA
    return pl.pallas_call(
        net_kernel,
        out_shape=jax.ShapeDtypeStruct((256, topics), f32),
        in_specs=[smem, vmem, vmem, anyw, anyw, vmem],
        out_specs=vmem,
        scratch_shapes=[
            pltpu.VMEM(tiles.shape, bf16),
            pltpu.VMEM(tiles.shape, bf16),
            pltpu.VMEM((8, 128), i32),
            pltpu.SMEM((8, 128), i32),
            pltpu.VMEM((16, 32, 128), f32),
            pltpu.VMEM((15, 4, 8, 128), f32),
            pltpu.VMEM((4, 8, 128), f32),
            pltpu.VMEM((7, 8, 128), f32),
            pltpu.VMEM((STREAMS, 16, 16, 128), f32),
            pltpu.VMEM((HOPS + 1, STREAMS, 3, 4, 16, 128), f32),
            pltpu.VMEM((STREAMS, 4, 16, 128), f32),
            pltpu.VMEM((STREAMS, 4, 16, 128), f32),
            *[pltpu.VMEM((4, 4, 4, 4, 16, 128), bf16) for _ in range(HOPS * STREAMS)],
            pltpu.VMEM((2, slots, 16, 128), f32),
            pltpu.VMEM((2, STREAMS, 2, 16, 128), f32),
            dma((2,)), dma((4,)), dma((4,)), dma((15,)), dma((15,)), dma((7,)), dma((7,)),
            dma((HOPS + 1, STREAMS, 3)), dma((HOPS + 1, STREAMS, 3)),
            dma((HOPS, STREAMS, 3, 18)), dma((HOPS, STREAMS, 3, 18)),
        ],
        compiler_params=pltpu.CompilerParams(
            collective_id=0, has_side_effects=True, vmem_limit_bytes=56 << 20
        ),
        name="spread",
    )(meta, local_topic, stage.reshape(16, 4, 8, 128), meta, tiles, member)


def solution(mesh):
    placed = (
        P(("hst", "doc"), None),
        P(),
        P(),
        P(("hst", "doc")),
        P(("hst", "doc"), None, None),
        P(("hst", "doc")),
        P(("hst", "doc")),
        P(("hst", "doc")),
        P("hst"),
    )
    return jax.shard_map(
        body, mesh=mesh, in_specs=placed, out_specs=P(("hst", "doc"), None), check_vma=False
    )
```

```python
import jax
import jax.numpy as jnp
from jax import lax
from jax.experimental import pallas as pl
from jax.experimental.pallas import tpu as pltpu
from jax.sharding import PartitionSpec as P

HOPS = 3
MESH = pl.DeviceIdType.MESH
NT = (((1,), (1,)), ((), ()))


def peer(dz, dx, dy, dc):
    h, d = lax.axis_index("hst"), lax.axis_index("doc")
    z = lax.rem(h // 4 + dz, 4)
    x = lax.rem(lax.rem(h, 4) + dx, 4)
    y = lax.rem(d // 2 + dy, 4)
    c = lax.rem(lax.rem(d, 2) + dc, 2)
    return (z * 4 + x, y * 2 + c)


PLANE = [(z, x, 0, 0) for z in range(4) for x in range(4) if z or x]
GROUP = [(0, 0, y, c) for y in range(4) for c in range(2) if y or c]
SIBLING = (0, 0, 0, 1)
STREAMS = 2
ORDERS = (
    (("x", "z", "y", 0, 1), ("z", "y", "x", 1, 2), ("y", "x", "z", 3, 1)),
    (("x", "z", "y", 0, 1), ("z", "y", "x", 1, 1), ("y", "x", "z", 2, 2)),
)


def order_tiles(dst_ref, src_ref, count, rows, meta):
    i32 = jnp.int32
    slots = dst_ref.shape[1]
    rows[...] = jnp.zeros_like(rows)
    rows[0:1, 0:slots] = dst_ref[...]
    rows[1:2, 0:slots] = src_ref[...]
    lane = lax.broadcasted_iota(i32, (128, 128), 1)
    sub = lax.broadcasted_iota(i32, (128, 128), 0)
    key = jnp.where(lane[0:1] < count, rows[0:1], jnp.where(lane[0:1] < slots, 16, 17))
    key_row = jnp.broadcast_to(key, (128, 128))
    key_col = jnp.transpose(key_row)
    src_col = jnp.transpose(jnp.broadcast_to(rows[1:2], (128, 128)))
    before = (key_row < key_col) | ((key_row == key_col) & (lane < sub))
    rank = jnp.sum(jnp.where(before, 1, 0), axis=1, keepdims=True)
    here = jnp.broadcast_to(rank, (128, 128)) == lane

    def down(value):
        return jnp.sum(value, axis=0, keepdims=True)

    perm = down(jnp.where(here, sub, 0))
    source = down(jnp.where(here, src_col, 0))
    sorted_key = down(jnp.where(here, key_col, 0))
    first = down(jnp.where(key_col < sorted_key, 1, 0))
    follows = jnp.where(lane[0:1] > first, 1, 0)
    upto = down(jnp.where(key_col <= lane, 1, 0))
    below = down(jnp.where(key_col < lane, 1, 0))
    some = jnp.where(upto > below, 1, 0)
    meta[0:1] = jnp.clip(perm, 0, slots - 1)
    meta[1:2] = jnp.clip(source, 0, 255)
    meta[2:3] = follows
    meta[3:4] = jnp.clip(upto - 1, 0, slots - 1)
    meta[4:5] = some


def split3(value):
    one = value.astype(jnp.bfloat16)
    rest = value - one.astype(jnp.float32)
    two = rest.astype(jnp.bfloat16)
    three = (rest - two.astype(jnp.float32)).astype(jnp.bfloat16)
    return one, two, three


def kernel(
    cnt_ref, dst_ref, src_ref, docs_ref, win_ref, wout_ref, dh_ref, tel_ref, tiles_any, out_ref,
    acc, lt, rows, meta, own_smem, sib_meta, sib_smem, own_tiles, sib_tiles, lt_in, stage, stage_in,
    group_sum, group_in, mass_own, mass_in, mass_sum, mass_all, part, rs_in,
    tele, state, g00, g01, g10, g11, g20, g21, runs, final,
    loc_sem, sib_send, sib_recv, st_send, st_recv, gr_send, gr_recv,
    ms_send, ms_recv, mg_send, mg_recv, rs_send, rs_recv, ag_send, ag_recv,
):
    step = pl.program_id(0)
    h, d = lax.axis_index("hst"), lax.axis_index("doc")
    pos = {"z": h // 4, "x": lax.rem(h, 4), "y": d // 2}
    core = lax.rem(d, 2)
    y = pos["y"]
    topics = wout_ref.shape[0]
    mine = pl.multiple_of(core * 32, 32)
    other = pl.multiple_of(32 - core * 32, 32)

    def remote(src, dst, send, recv, to):
        return pltpu.make_async_remote_copy(
            src_ref=src, dst_ref=dst, send_sem=send, recv_sem=recv, device_id=peer(*to), device_id_type=MESH
        )

    def wait_bytes(ref, sem):
        pltpu.make_async_copy(ref, ref, sem).wait()

    own_copy = pltpu.make_async_copy(tiles_any, own_tiles, loc_sem.at[0])
    meta_own = pltpu.make_async_copy(meta, own_smem, loc_sem.at[1])
    meta_local = pltpu.make_async_copy(sib_meta, sib_smem, loc_sem.at[2])
    meta_copy = remote(meta, sib_meta, sib_send.at[1], sib_recv.at[1], SIBLING)
    tile_copy = remote(own_tiles, sib_tiles, sib_send.at[2], sib_recv.at[2], SIBLING)
    stage_copies = [
        remote(stage.at[peer(*to)[0]], stage_in.at[j], st_send, st_recv, to)
        for j, to in enumerate(PLANE)
    ]
    group_copies = [
        remote(group_sum.at[peer(*to)[1] // 2], group_in.at[j], gr_send, gr_recv, to)
        for j, to in enumerate(GROUP)
    ]
    mass_copies = [
        remote(mass_own, mass_in.at[j], ms_send, ms_recv, to) for j, to in enumerate(PLANE)
    ]
    total_copies = [
        remote(mass_sum, mass_all.at[j], mg_send, mg_recv, to) for j, to in enumerate(GROUP)
    ]

    @pl.when(step == 0)
    def _():
        barrier = pltpu.get_barrier_semaphore()
        for to in PLANE + GROUP:
            pl.semaphore_signal(barrier, inc=1, device_id=peer(*to), device_id_type=MESH)
        own_copy.start()
        acc[...] = jnp.zeros_like(acc)
        order_tiles(dst_ref, src_ref, cnt_ref[0], rows, meta)
        meta_own.start()
        own_copy.wait()

    @pl.when(step == 2)
    def _():
        pl.semaphore_wait(pltpu.get_barrier_semaphore(), len(PLANE) + len(GROUP))
        meta_copy.start()
        tile_copy.start()
        slots = own_tiles.shape[0]
        colsum = jnp.sum(own_tiles[...].astype(jnp.float32), axis=1)
        row = lax.broadcasted_iota(jnp.int32, (512, slots), 0)
        src = src_ref[...]
        used = lax.broadcasted_iota(jnp.int32, (1, slots), 1) < cnt_ref[0]
        spot = jnp.where(used, (src // 4) * 8 + src % 4, 7)
        onehot = jnp.where(row == spot, 1.0, 0.0).astype(jnp.bfloat16)
        degree = sum(jnp.dot(onehot, p, preferred_element_type=jnp.float32) for p in split3(colsum))
        stage[...] = degree.reshape(16, 4, 8, 128)
        for copy in stage_copies:
            copy.start()

    @pl.when(step == 4)
    def _():
        wait_bytes(stage_in, st_recv)
        total = stage[h]
        for j in range(len(PLANE)):
            total += stage_in[j]
        group_sum[...] = total
        for copy in group_copies:
            copy.start()
        wait_bytes(stage_in, st_send)
        meta_copy.wait()
        meta_local.start()

    owner = dh_ref[0]
    upper = jnp.where(owner >= 1024, 1.0, 0.0).astype(jnp.bfloat16)
    lower = jnp.where(owner >= 1024, 0.0, 1.0).astype(jnp.bfloat16)
    pts = []
    for c in range(0, docs_ref.shape[0], 1024):
        hidden = jax.nn.gelu(
            jnp.dot(docs_ref[c:c+1024], win_ref[...], preferred_element_type=jnp.float32), approximate=True
        ).astype(jnp.bfloat16)
        logits = lax.dot_general(wout_ref[...], hidden, NT, preferred_element_type=jnp.float32)
        weight = jnp.exp(logits - jnp.max(logits, axis=0, keepdims=True))
        probs = weight / jnp.sum(weight, axis=0, keepdims=True)
        high = probs.astype(jnp.bfloat16)
        low = (probs - high.astype(jnp.float32)).astype(jnp.bfloat16)
        both = jnp.concatenate([high, low], axis=0)
        pts.append(jnp.concatenate([both * lower[:, c:c+1024], both * upper[:, c:c+1024]], axis=0))
    pt = jnp.concatenate(pts, axis=1)
    spot = (owner & 1023)
    piece = 512
    for at in range(0, 1024, piece):
        row = (lax.broadcasted_iota(jnp.int32, (piece, owner.shape[1]), 0) + at)
        onehot = jnp.where(row == spot, 1.0, 0.0).astype(jnp.bfloat16)
        acc[at : at + piece] += lax.dot_general(onehot, pt, NT, preferred_element_type=jnp.float32)

    @pl.when(step == pl.num_programs(0) - 1)
    def _():
        mass = jnp.zeros((topics, 128), jnp.float32)
        for b in range(16):
            flat = jnp.transpose(acc[b % 8 * 128 : (b % 8 + 1) * 128, b // 8 * 128 : (b // 8 + 1) * 128])
            flat = flat[:topics] + flat[topics:]
            lt[b] = flat
            mass += flat * tel_ref[b : b + 1, :].astype(jnp.float32)
        lt_copy = remote(lt.at[:, pl.ds(other, 32), :], lt_in, sib_send.at[0], sib_recv.at[0], SIBLING)
        lt_copy.start()
        wide = jnp.concatenate([mass, jnp.zeros_like(mass)], axis=0)
        mass_own[...] = jnp.broadcast_to(jnp.sum(jnp.transpose(wide), axis=0, keepdims=True), (8, 128))
        for copy in mass_copies:
            copy.start()
        wait_bytes(group_in, gr_recv)
        total = group_sum[y]
        for j in range(len(GROUP)):
            total += group_in[j]
        inverse = (1.0 / jnp.maximum(total[0:4], 1.0))[:, None, :]

        def reduce_start(inst, s):
            copies = []
            for k in range(1, 4):
                there = lax.rem(y + k, 4)
                copies.append(
                    remote(
                        part.at[s, pl.ds(there * 4, 4)], rs_in.at[inst, s, k - 1],
                        rs_send.at[inst, s], rs_recv.at[inst, s], (0, 0, k, 0),
                    )
                )
            for copy in copies:
                copy.start()

        def reduce_end(inst, s):
            wait_bytes(rs_in.at[inst, s], rs_recv.at[inst, s])
            total = part[s, pl.ds(y * 4, 4)] + rs_in[inst, s, 0] + rs_in[inst, s, 1] + rs_in[inst, s, 2]
            wait_bytes(rs_in.at[inst, s], rs_send.at[inst, s])
            return total

        lt_copy.wait_recv()
        for s in range(STREAMS):
            at = pl.multiple_of(core * 32 + s * 16, 16)
            part[s] = lt[:, pl.ds(at, 16), :] + lt_in[:, s * 16 : s * 16 + 16]
            reduce_start(0, s)

        wait_bytes(mass_in, ms_recv)
        total = mass_own[...]
        for j in range(len(PLANE)):
            total += mass_in[j]
        mass_sum[...] = total
        for copy in total_copies:
            copy.start()

        lt_copy.wait_send()
        wait_bytes(group_in, gr_send)
        wait_bytes(mass_in, ms_send)
        topic = [reduce_end(0, s) for s in range(STREAMS)]
        wait_bytes(mass_all, mg_recv)
        total = mass_sum[...]
        for j in range(len(GROUP)):
            total += mass_all[j]
        square = jnp.transpose(jnp.broadcast_to(total[0:1], (128, 128)))
        mass = jnp.where(core == 0, square[0:32], square[32:64])
        member = tel_ref[pl.ds(y * 4, 4), :].astype(jnp.float32)[:, None, :]
        for s in range(STREAMS):
            start = member * topic[s] / mass[None, s * 16 : s * 16 + 16]
            tele[s] = start
            state[s] = start
        wait_bytes(mass_all, mg_send)
        meta_own.wait()
        meta_local.wait()
        tile_copy.wait()

        def along(axis, k):
            return tuple(k if axis == name else 0 for name in "zxy") + (0,)

        class Stream:
            def __init__(self, hop, s, gathered):
                self.hop, self.s, self.gathered = hop, s, gathered

            def place(self, fixed, first, count):
                index = [fixed[axis] if axis in fixed else slice(None) for axis in "zxy"]
                return self.gathered.at[(*index, pl.ds(first, count))]

            def send(self, slot, axis, k, ref):
                at = (self.hop, self.s)
                copy = remote(ref, ref, ag_send.at[at], ag_recv.at[(*at, slot)], along(axis, k))
                copy.start()
                return copy

            def stage1(self):
                sent = (state[self.s] * inverse).astype(jnp.bfloat16)
                self.gathered[pos["z"], pos["x"], y] = sent
                for o, (a1, a2, a3, first, count) in enumerate(ORDERS[self.s]):
                    ref = self.place(pos, first, count)
                    for k in range(1, 4):
                        self.send(o, a1, k, ref)

            def stage2(self):
                self.two = []
                for o, (a1, a2, a3, first, count) in enumerate(ORDERS[self.s]):
                    wait_bytes(self.gathered.at[0, 0, pl.ds(0, 3), pl.ds(0, count)], ag_recv.at[self.hop, self.s, o])
                    ref = self.place({a2: pos[a2], a3: pos[a3]}, first, count)
                    self.two.append([self.send(3 * o + 2 + k, a2, k, ref) for k in range(1, 4)])
                    for k in range(1, 4):
                        self.send(12, a3, k, ref)

            def stage3(self):
                for k2 in (1, 3, 2):
                    for o, (a1, a2, a3, first, count) in enumerate(ORDERS[self.s]):
                        self.two[o][k2 - 1].wait_recv()
                        there = lax.rem(pos[a2] + 4 - k2, 4)
                        ref = self.place({a2: there, a3: pos[a3]}, first, count)
                        for k in range(1, 4):
                            self.send(12, a3, k, ref)

            def multiply(self):
                wait_bytes(runs.at[:, pl.ds(0, 48)], ag_recv.at[self.hop, self.s, 12])
                lists = ((own_smem, own_tiles), (sib_smem, sib_tiles))
                batch = 32
                gathered, s = self.gathered, self.s

                def tile_body(i, run):
                    run = list(run)
                    for j in range(batch):
                        r = i * batch + j
                        for n, (m, t) in enumerate(lists):
                            b = m[1, r]
                            slab = gathered[b // 64, (b // 16) % 4, (b // 4) % 4, b % 4]
                            prod = lax.dot_general(slab, t[m[0, r]], NT, preferred_element_type=jnp.float32)
                            run[n] = jnp.where(m[2, r] > 0, run[n], 0.0) + prod
                            runs[n, r] = run[n]
                    return tuple(run)

                zero = jnp.zeros((16, 128), jnp.float32)
                lax.fori_loop(0, own_tiles.shape[0] // batch, tile_body, (zero, zero))
                for blk in range(16):
                    value = zero
                    for n, (m, t) in enumerate(lists):
                        value += jnp.where(m[4, blk] > 0, runs[n, m[3, blk]], 0.0)
                    part[s, blk] = value
                reduce_start(self.hop + 1, s)

            def finish(self):
                inflow = reduce_end(self.hop + 1, self.s)
                state[self.s] = 0.85 * inflow + 0.15 * tele[self.s]

            def settle(self):
                wait_bytes(runs.at[:, pl.ds(0, 63)], ag_send.at[self.hop, self.s])

        streams = [[Stream(hop, s, g) for s, g in enumerate(gs)] for hop, gs in enumerate(((g00, g01), (g10, g11), (g20, g21)))]
        for one in streams[0]:
            one.stage1()
        for hop in range(HOPS):
            for one in streams[hop]:
                one.stage2()
            for one in streams[hop]:
                one.stage3()
            for one in streams[hop]:
                one.multiply()
            for s, one in enumerate(streams[hop]):
                one.finish()
                if hop + 1 < HOPS:
                    streams[hop + 1][s].stage1()
            for one in streams[hop]:
                one.settle()

        hosts_all = 128.0 * 256.0
        keep = pl.multiple_of(core * 2, 2)
        give = pl.multiple_of(2 - core * 2, 2)
        state[...] = hosts_all * state[...]
        last = remote(state.at[:, pl.ds(give, 2)], final.at[core], sib_send.at[3], sib_recv.at[3], SIBLING)
        last.start()
        final[core] = state[:, pl.ds(keep, 2)]
        last.wait()
        for j in range(2):
            out_ref[j * 128 : (j + 1) * 128, :] = jnp.transpose(final[:, :, j].reshape(64, 128))


def body(docs, w_in, w_out, doc_host, tiles, dst_block, src_block, tile_count, teleport):
    f32, bf16, i32 = jnp.float32, jnp.bfloat16, jnp.int32
    docs_dev, depth = docs.shape
    hidden, topics = w_out.shape
    slots = tiles.shape[0]
    steps = 8
    rows = docs_dev // steps

    def whole(*shape):
        return pl.BlockSpec(shape, lambda i: (0,) * len(shape))

    dma = pltpu.SemaphoreType.DMA
    return pl.pallas_call(
        kernel,
        grid=(steps,),
        out_shape=jax.ShapeDtypeStruct((256, topics), f32),
        in_specs=[
            pl.BlockSpec(memory_space=pltpu.SMEM),
            whole(1, slots),
            whole(1, slots),
            pl.BlockSpec((rows, depth), lambda i: (i, 0)),
            whole(depth, hidden),
            whole(topics, hidden),
            pl.BlockSpec((1, 1, rows), lambda i: (i, 0, 0)),
            whole(16, 128),
            pl.BlockSpec(memory_space=pl.ANY),
        ],
        out_specs=whole(256, topics),
        scratch_shapes=[
            pltpu.VMEM((1024, 256), f32),
            pltpu.VMEM((16, topics, 128), f32),
            pltpu.VMEM((8, 128), i32),
            pltpu.VMEM((8, 128), i32),
            pltpu.SMEM((8, 128), i32),
            pltpu.VMEM((8, 128), i32),
            pltpu.SMEM((8, 128), i32),
            pltpu.VMEM(tiles.shape, bf16),
            pltpu.VMEM(tiles.shape, bf16),
            pltpu.VMEM((16, 32, 128), f32),
            pltpu.VMEM((16, 4, 8, 128), f32),
            pltpu.VMEM((15, 4, 8, 128), f32),
            pltpu.VMEM((4, 8, 128), f32),
            pltpu.VMEM((7, 8, 128), f32),
            pltpu.VMEM((8, 128), f32),
            pltpu.VMEM((15, 8, 128), f32),
            pltpu.VMEM((8, 128), f32),
            pltpu.VMEM((7, 8, 128), f32),
            pltpu.VMEM((STREAMS, 16, 16, 128), f32),
            pltpu.VMEM((HOPS + 1, STREAMS, 3, 4, 16, 128), f32),
            pltpu.VMEM((STREAMS, 4, 16, 128), f32),
            pltpu.VMEM((STREAMS, 4, 16, 128), f32),
            *[pltpu.VMEM((4, 4, 4, 4, 16, 128), bf16) for _ in range(HOPS * STREAMS)],
            pltpu.VMEM((2, slots, 16, 128), f32),
            pltpu.VMEM((2, STREAMS, 2, 16, 128), f32),
            dma((3,)), dma((4,)), dma((4,)), *[dma] * 8,
            dma((HOPS + 1, STREAMS)), dma((HOPS + 1, STREAMS)), dma((HOPS, STREAMS)), dma((HOPS, STREAMS, 13)),
        ],
        compiler_params=pltpu.CompilerParams(
            collective_id=0, has_side_effects=True, vmem_limit_bytes=58 << 20
        ),
        name="spread",
    )(
        tile_count, dst_block.reshape(1, slots), src_block.reshape(1, slots), docs, w_in, w_out.T,
        doc_host.reshape(steps, 1, rows), teleport.reshape(16, 128), tiles,
    )


def solution(mesh):
    placed = (
        P(("hst", "doc"), None),
        P(),
        P(),
        P(("hst", "doc")),
        P(("hst", "doc"), None, None),
        P(("hst", "doc")),
        P(("hst", "doc")),
        P(("hst", "doc")),
        P("hst"),
    )
    return jax.shard_map(
        body, mesh=mesh, in_specs=placed, out_specs=P(("hst", "doc"), None), check_vma=False
    )
```

```python
import jax
import jax.numpy as jnp
from jax import lax
from jax.experimental import pallas as pl
from jax.experimental.pallas import tpu as pltpu
from jax.sharding import PartitionSpec as P

HOPS = 3
MESH = pl.DeviceIdType.MESH
NT = (((1,), (1,)), ((), ()))


def peer(dz, dx, dy, dc):
    h, d = lax.axis_index("hst"), lax.axis_index("doc")
    z = lax.rem(h // 4 + dz, 4)
    x = lax.rem(lax.rem(h, 4) + dx, 4)
    y = lax.rem(d // 2 + dy, 4)
    c = lax.rem(lax.rem(d, 2) + dc, 2)
    return (z * 4 + x, y * 2 + c)


PLANE = [(z, x, 0, 0) for z in range(4) for x in range(4) if z or x]
GROUP = [(0, 0, y, c) for y in range(4) for c in range(2) if y or c]
SIBLING = (0, 0, 0, 1)
STREAMS = 2
ORDERS = (
    (("x", "z", "y", 0, 1), ("z", "y", "x", 1, 2), ("y", "x", "z", 3, 1)),
    (("x", "z", "y", 0, 1), ("z", "y", "x", 1, 1), ("y", "x", "z", 2, 2)),
)


def order_tiles(dst_ref, src_ref, count, rows, meta):
    i32 = jnp.int32
    slots = dst_ref.shape[1]
    rows[...] = jnp.zeros_like(rows)
    rows[0:1, 0:slots] = dst_ref[...]
    rows[1:2, 0:slots] = src_ref[...]
    lane = lax.broadcasted_iota(i32, (128, 128), 1)
    sub = lax.broadcasted_iota(i32, (128, 128), 0)
    key = jnp.where(lane[0:1] < count, rows[0:1], jnp.where(lane[0:1] < slots, 16, 17))
    key_row = jnp.broadcast_to(key, (128, 128))
    key_col = jnp.transpose(key_row)
    src_col = jnp.transpose(jnp.broadcast_to(rows[1:2], (128, 128)))
    before = (key_row < key_col) | ((key_row == key_col) & (lane < sub))
    rank = jnp.sum(jnp.where(before, 1, 0), axis=1, keepdims=True)
    here = jnp.broadcast_to(rank, (128, 128)) == lane

    def down(value):
        return jnp.sum(value, axis=0, keepdims=True)

    perm = down(jnp.where(here, sub, 0))
    source = down(jnp.where(here, src_col, 0))
    sorted_key = down(jnp.where(here, key_col, 0))
    first = down(jnp.where(key_col < sorted_key, 1, 0))
    follows = jnp.where(lane[0:1] > first, 1, 0)
    upto = down(jnp.where(key_col <= lane, 1, 0))
    below = down(jnp.where(key_col < lane, 1, 0))
    some = jnp.where(upto > below, 1, 0)
    meta[0:1] = jnp.clip(perm, 0, slots - 1)
    meta[1:2] = jnp.clip(source, 0, 255)
    meta[2:3] = follows
    meta[3:4] = jnp.clip(upto - 1, 0, slots - 1)
    meta[4:5] = some


def split3(value):
    one = value.astype(jnp.bfloat16)
    rest = value - one.astype(jnp.float32)
    two = rest.astype(jnp.bfloat16)
    three = (rest - two.astype(jnp.float32)).astype(jnp.bfloat16)
    return one, two, three


def kernel(
    cnt_ref, dst_ref, src_ref, docs_ref, win_ref, wout_ref, dh_ref, tel_ref, tiles_any, out_ref,
    acc, lt, rows, meta, own_smem, sib_meta, sib_smem, raw_tiles, own_tiles, sib_tiles, lt_in, stage, stage_in,
    group_sum, group_in, mass_own, mass_in, mass_sum, mass_all, part, rs_in,
    tele, state, g00, g01, g10, g11, g20, g21, runs, final,
    loc_sem, sib_send, sib_recv, st_send, st_recv, gr_send, gr_recv,
    ms_send, ms_recv, mg_send, mg_recv, rs_send, rs_recv, ag_send, ag_recv,
):
    step = pl.program_id(0)
    h, d = lax.axis_index("hst"), lax.axis_index("doc")
    pos = {"z": h // 4, "x": lax.rem(h, 4), "y": d // 2}
    core = lax.rem(d, 2)
    y = pos["y"]
    topics = wout_ref.shape[0]
    mine = pl.multiple_of(core * 32, 32)
    other = pl.multiple_of(32 - core * 32, 32)

    def remote(src, dst, send, recv, to):
        return pltpu.make_async_remote_copy(
            src_ref=src, dst_ref=dst, send_sem=send, recv_sem=recv, device_id=peer(*to), device_id_type=MESH
        )

    def wait_bytes(ref, sem):
        pltpu.make_async_copy(ref, ref, sem).wait()

    own_copy = pltpu.make_async_copy(tiles_any, raw_tiles, loc_sem.at[0])
    meta_own = pltpu.make_async_copy(meta, own_smem, loc_sem.at[1])
    meta_local = pltpu.make_async_copy(sib_meta, sib_smem, loc_sem.at[2])
    meta_copy = remote(meta, sib_meta, sib_send.at[1], sib_recv.at[1], SIBLING)
    tile_copy = remote(own_tiles, sib_tiles, sib_send.at[2], sib_recv.at[2], SIBLING)
    stage_copies = [
        remote(stage.at[peer(*to)[0]], stage_in.at[j], st_send, st_recv, to)
        for j, to in enumerate(PLANE)
    ]
    group_copies = [
        remote(group_sum.at[peer(*to)[1] // 2], group_in.at[j], gr_send, gr_recv, to)
        for j, to in enumerate(GROUP)
    ]
    mass_copies = [
        remote(mass_own, mass_in.at[j], ms_send, ms_recv, to) for j, to in enumerate(PLANE)
    ]
    total_copies = [
        remote(mass_sum, mass_all.at[j], mg_send, mg_recv, to) for j, to in enumerate(GROUP)
    ]

    def flip_tiles():
        def flip(i, carry):
            for j in range(8):
                own_tiles[i * 8 + j] = jnp.transpose(raw_tiles[i * 8 + j])
            return carry

        lax.fori_loop(0, own_tiles.shape[0] // 8, flip, 0)

    @pl.when(step == 0)
    def _():
        barrier = pltpu.get_barrier_semaphore()
        for to in PLANE + GROUP:
            pl.semaphore_signal(barrier, inc=1, device_id=peer(*to), device_id_type=MESH)
        own_copy.start()
        acc[...] = jnp.zeros_like(acc)
        order_tiles(dst_ref, src_ref, cnt_ref[0], rows, meta)
        meta_own.start()

    @pl.when(step == 1)
    def _():
        own_copy.wait()
        flip_tiles()

    @pl.when(step == 2)
    def _():
        pl.semaphore_wait(pltpu.get_barrier_semaphore(), len(PLANE) + len(GROUP))
        meta_copy.start()
        tile_copy.start()
        slots = own_tiles.shape[0]
        colsum = jnp.sum(raw_tiles[...].astype(jnp.float32), axis=1)
        row = lax.broadcasted_iota(jnp.int32, (512, slots), 0)
        src = src_ref[...]
        used = lax.broadcasted_iota(jnp.int32, (1, slots), 1) < cnt_ref[0]
        spot = jnp.where(used, (src // 4) * 8 + src % 4, 7)
        onehot = jnp.where(row == spot, 1.0, 0.0).astype(jnp.bfloat16)
        degree = sum(jnp.dot(onehot, p, preferred_element_type=jnp.float32) for p in split3(colsum))
        stage[...] = degree.reshape(16, 4, 8, 128)
        for copy in stage_copies:
            copy.start()

    @pl.when(step == 4)
    def _():
        wait_bytes(stage_in, st_recv)
        total = stage[h]
        for j in range(len(PLANE)):
            total += stage_in[j]
        group_sum[...] = total
        for copy in group_copies:
            copy.start()
        wait_bytes(stage_in, st_send)
        meta_copy.wait()
        meta_local.start()

    owner = dh_ref[0]
    upper = jnp.where(owner >= 1024, 1.0, 0.0).astype(jnp.bfloat16)
    lower = jnp.where(owner >= 1024, 0.0, 1.0).astype(jnp.bfloat16)
    pts = []
    for c in range(0, docs_ref.shape[0], 1024):
        hidden = jax.nn.gelu(
            jnp.dot(docs_ref[c:c+1024], win_ref[...], preferred_element_type=jnp.float32), approximate=True
        ).astype(jnp.bfloat16)
        logits = lax.dot_general(wout_ref[...], hidden, NT, preferred_element_type=jnp.float32)
        weight = jnp.exp(logits - jnp.max(logits, axis=0, keepdims=True))
        probs = weight / jnp.sum(weight, axis=0, keepdims=True)
        high = probs.astype(jnp.bfloat16)
        low = (probs - high.astype(jnp.float32)).astype(jnp.bfloat16)
        both = jnp.concatenate([high, low], axis=0)
        pts.append(jnp.concatenate([both * lower[:, c:c+1024], both * upper[:, c:c+1024]], axis=0))
    pt = jnp.concatenate(pts, axis=1)
    spot = (owner & 1023)
    piece = 512
    for at in range(0, 1024, piece):
        row = (lax.broadcasted_iota(jnp.int32, (piece, owner.shape[1]), 0) + at)
        onehot = jnp.where(row == spot, 1.0, 0.0).astype(jnp.bfloat16)
        acc[at : at + piece] += lax.dot_general(onehot, pt, NT, preferred_element_type=jnp.float32)

    @pl.when(step == pl.num_programs(0) - 1)
    def _():
        mass = jnp.zeros((topics, 128), jnp.float32)
        for b in range(16):
            flat = jnp.transpose(acc[b % 8 * 128 : (b % 8 + 1) * 128, b // 8 * 128 : (b // 8 + 1) * 128])
            flat = flat[:topics] + flat[topics:]
            lt[b] = flat
            mass += flat * tel_ref[b : b + 1, :].astype(jnp.float32)
        lt_copy = remote(lt.at[:, pl.ds(other, 32), :], lt_in, sib_send.at[0], sib_recv.at[0], SIBLING)
        lt_copy.start()
        wide = jnp.concatenate([mass, jnp.zeros_like(mass)], axis=0)
        mass_own[...] = jnp.broadcast_to(jnp.sum(jnp.transpose(wide), axis=0, keepdims=True), (8, 128))
        for copy in mass_copies:
            copy.start()
        wait_bytes(group_in, gr_recv)
        total = group_sum[y]
        for j in range(len(GROUP)):
            total += group_in[j]
        inverse = (1.0 / jnp.maximum(total[0:4], 1.0))[:, None, :]

        def reduce_start(inst, s):
            copies = []
            for k in range(1, 4):
                there = lax.rem(y + k, 4)
                copies.append(
                    remote(
                        part.at[s, pl.ds(there * 4, 4)], rs_in.at[inst, s, k - 1],
                        rs_send.at[inst, s], rs_recv.at[inst, s], (0, 0, k, 0),
                    )
                )
            for copy in copies:
                copy.start()

        def reduce_end(inst, s):
            wait_bytes(rs_in.at[inst, s], rs_recv.at[inst, s])
            total = part[s, pl.ds(y * 4, 4)] + rs_in[inst, s, 0] + rs_in[inst, s, 1] + rs_in[inst, s, 2]
            wait_bytes(rs_in.at[inst, s], rs_send.at[inst, s])
            return total

        lt_copy.wait_recv()
        for s in range(STREAMS):
            at = pl.multiple_of(core * 32 + s * 16, 16)
            part[s] = lt[:, pl.ds(at, 16), :] + lt_in[:, s * 16 : s * 16 + 16]
            reduce_start(0, s)

        wait_bytes(mass_in, ms_recv)
        total = mass_own[...]
        for j in range(len(PLANE)):
            total += mass_in[j]
        mass_sum[...] = total
        for copy in total_copies:
            copy.start()

        lt_copy.wait_send()
        wait_bytes(group_in, gr_send)
        wait_bytes(mass_in, ms_send)
        topic = [reduce_end(0, s) for s in range(STREAMS)]
        wait_bytes(mass_all, mg_recv)
        total = mass_sum[...]
        for j in range(len(GROUP)):
            total += mass_all[j]
        square = jnp.transpose(jnp.broadcast_to(total[0:1], (128, 128)))
        mass = jnp.where(core == 0, square[0:32], square[32:64])
        member = tel_ref[pl.ds(y * 4, 4), :].astype(jnp.float32)[:, None, :]
        for s in range(STREAMS):
            start = member * topic[s] / mass[None, s * 16 : s * 16 + 16]
            tele[s] = start
            state[s] = start
        wait_bytes(mass_all, mg_send)
        meta_own.wait()
        meta_local.wait()
        tile_copy.wait()

        def along(axis, k):
            return tuple(k if axis == name else 0 for name in "zxy") + (0,)

        class Stream:
            def __init__(self, hop, s, gathered):
                self.hop, self.s, self.gathered = hop, s, gathered

            def place(self, fixed, first, count):
                index = [fixed[axis] if axis in fixed else slice(None) for axis in "zxy"]
                return self.gathered.at[(*index, pl.ds(first, count))]

            def send(self, slot, axis, k, ref):
                at = (self.hop, self.s)
                copy = remote(ref, ref, ag_send.at[at], ag_recv.at[(*at, slot)], along(axis, k))
                copy.start()
                return copy

            def stage1(self):
                sent = (state[self.s] * inverse).astype(jnp.bfloat16)
                self.gathered[pos["z"], pos["x"], y] = sent
                for o, (a1, a2, a3, first, count) in enumerate(ORDERS[self.s]):
                    ref = self.place(pos, first, count)
                    for k in range(1, 4):
                        self.send(o, a1, k, ref)

            def stage2(self):
                self.two = []
                for o, (a1, a2, a3, first, count) in enumerate(ORDERS[self.s]):
                    wait_bytes(self.gathered.at[0, 0, pl.ds(0, 3), pl.ds(0, count)], ag_recv.at[self.hop, self.s, o])
                    ref = self.place({a2: pos[a2], a3: pos[a3]}, first, count)
                    self.two.append([self.send(3 * o + 2 + k, a2, k, ref) for k in range(1, 4)])
                    for k in range(1, 4):
                        self.send(12, a3, k, ref)

            def stage3(self):
                for k2 in (1, 3, 2):
                    for o, (a1, a2, a3, first, count) in enumerate(ORDERS[self.s]):
                        self.two[o][k2 - 1].wait_recv()
                        there = lax.rem(pos[a2] + 4 - k2, 4)
                        ref = self.place({a2: there, a3: pos[a3]}, first, count)
                        for k in range(1, 4):
                            self.send(12, a3, k, ref)

            def multiply(self):
                wait_bytes(runs.at[:, pl.ds(0, 48)], ag_recv.at[self.hop, self.s, 12])
                lists = ((own_smem, own_tiles), (sib_smem, sib_tiles))
                batch = 64
                gathered, s = self.gathered, self.s

                def tile_body(i, run):
                    run = list(run)
                    for j in range(batch):
                        r = i * batch + j
                        for n, (m, t) in enumerate(lists):
                            b = m[1, r]
                            slab = gathered[b >> 6, (b >> 4) & 3, (b >> 2) & 3, b & 3]
                            prod = jnp.dot(slab, t[m[0, r]], preferred_element_type=jnp.float32)
                            run[n] = jnp.where(m[2, r] > 0, run[n], 0.0) + prod
                            runs[n, r] = run[n]
                    return tuple(run)

                zero = jnp.zeros((16, 128), jnp.float32)
                lax.fori_loop(0, own_tiles.shape[0] // batch, tile_body, (zero, zero))
                for blk in range(16):
                    value = zero
                    for n, (m, t) in enumerate(lists):
                        value += jnp.where(m[4, blk] > 0, runs[n, m[3, blk]], 0.0)
                    part[s, blk] = value
                reduce_start(self.hop + 1, s)

            def finish(self):
                inflow = reduce_end(self.hop + 1, self.s)
                state[self.s] = 0.85 * inflow + 0.15 * tele[self.s]

            def settle(self):
                wait_bytes(runs.at[:, pl.ds(0, 63)], ag_send.at[self.hop, self.s])

        streams = [[Stream(hop, s, g) for s, g in enumerate(gs)] for hop, gs in enumerate(((g00, g01), (g10, g11), (g20, g21)))]
        for one in streams[0]:
            one.stage1()
        for hop in range(HOPS):
            for one in streams[hop]:
                one.stage2()
            for one in streams[hop]:
                one.stage3()
            for one in streams[hop]:
                one.multiply()
            for s, one in enumerate(streams[hop]):
                one.finish()
                if hop + 1 < HOPS:
                    streams[hop + 1][s].stage1()
            for one in streams[hop]:
                one.settle()

        hosts_all = 128.0 * 256.0
        keep = pl.multiple_of(core * 2, 2)
        give = pl.multiple_of(2 - core * 2, 2)
        state[...] = hosts_all * state[...]
        last = remote(state.at[:, pl.ds(give, 2)], final.at[core], sib_send.at[3], sib_recv.at[3], SIBLING)
        last.start()
        final[core] = state[:, pl.ds(keep, 2)]
        last.wait()
        for j in range(2):
            out_ref[j * 128 : (j + 1) * 128, :] = jnp.transpose(final[:, :, j].reshape(64, 128))


def body(docs, w_in, w_out, doc_host, tiles, dst_block, src_block, tile_count, teleport):
    f32, bf16, i32 = jnp.float32, jnp.bfloat16, jnp.int32
    docs_dev, depth = docs.shape
    hidden, topics = w_out.shape
    slots = tiles.shape[0]
    steps = 8
    rows = docs_dev // steps

    def whole(*shape):
        return pl.BlockSpec(shape, lambda i: (0,) * len(shape))

    dma = pltpu.SemaphoreType.DMA
    return pl.pallas_call(
        kernel,
        grid=(steps,),
        out_shape=jax.ShapeDtypeStruct((256, topics), f32),
        in_specs=[
            pl.BlockSpec(memory_space=pltpu.SMEM),
            whole(1, slots),
            whole(1, slots),
            pl.BlockSpec((rows, depth), lambda i: (i, 0)),
            whole(depth, hidden),
            whole(topics, hidden),
            pl.BlockSpec((1, 1, rows), lambda i: (i, 0, 0)),
            whole(16, 128),
            pl.BlockSpec(memory_space=pl.ANY),
        ],
        out_specs=whole(256, topics),
        scratch_shapes=[
            pltpu.VMEM((1024, 256), f32),
            pltpu.VMEM((16, topics, 128), f32),
            pltpu.VMEM((8, 128), i32),
            pltpu.VMEM((8, 128), i32),
            pltpu.SMEM((8, 128), i32),
            pltpu.VMEM((8, 128), i32),
            pltpu.SMEM((8, 128), i32),
            pltpu.VMEM(tiles.shape, bf16),
            pltpu.VMEM(tiles.shape, bf16),
            pltpu.VMEM(tiles.shape, bf16),
            pltpu.VMEM((16, 32, 128), f32),
            pltpu.VMEM((16, 4, 8, 128), f32),
            pltpu.VMEM((15, 4, 8, 128), f32),
            pltpu.VMEM((4, 8, 128), f32),
            pltpu.VMEM((7, 8, 128), f32),
            pltpu.VMEM((8, 128), f32),
            pltpu.VMEM((15, 8, 128), f32),
            pltpu.VMEM((8, 128), f32),
            pltpu.VMEM((7, 8, 128), f32),
            pltpu.VMEM((STREAMS, 16, 16, 128), f32),
            pltpu.VMEM((HOPS + 1, STREAMS, 3, 4, 16, 128), f32),
            pltpu.VMEM((STREAMS, 4, 16, 128), f32),
            pltpu.VMEM((STREAMS, 4, 16, 128), f32),
            *[pltpu.VMEM((4, 4, 4, 4, 16, 128), bf16) for _ in range(HOPS * STREAMS)],
            pltpu.VMEM((2, slots, 16, 128), f32),
            pltpu.VMEM((2, STREAMS, 2, 16, 128), f32),
            dma((3,)), dma((4,)), dma((4,)), *[dma] * 8,
            dma((HOPS + 1, STREAMS)), dma((HOPS + 1, STREAMS)), dma((HOPS, STREAMS)), dma((HOPS, STREAMS, 13)),
        ],
        compiler_params=pltpu.CompilerParams(
            collective_id=0, has_side_effects=True, vmem_limit_bytes=58 << 20
        ),
        name="spread",
    )(
        tile_count, dst_block.reshape(1, slots), src_block.reshape(1, slots), docs, w_in, w_out.T,
        doc_host.reshape(steps, 1, rows), teleport.reshape(16, 128), tiles,
    )


def solution(mesh):
    placed = (
        P(("hst", "doc"), None),
        P(),
        P(),
        P(("hst", "doc")),
        P(("hst", "doc"), None, None),
        P(("hst", "doc")),
        P(("hst", "doc")),
        P(("hst", "doc")),
        P("hst"),
    )
    return jax.shard_map(
        body, mesh=mesh, in_specs=placed, out_specs=P(("hst", "doc"), None), check_vma=False
    )
```

```python
import jax
import jax.numpy as jnp
from jax import lax
from jax.experimental import pallas as pl
from jax.experimental.pallas import tpu as pltpu
from jax.sharding import PartitionSpec as P

HOPS = 3
MESH = pl.DeviceIdType.MESH
NT = (((1,), (1,)), ((), ()))


def peer(dz, dx, dy, dc):
    h, d = lax.axis_index("hst"), lax.axis_index("doc")
    z = lax.rem(h // 4 + dz, 4)
    x = lax.rem(lax.rem(h, 4) + dx, 4)
    y = lax.rem(d // 2 + dy, 4)
    c = lax.rem(lax.rem(d, 2) + dc, 2)
    return (z * 4 + x, y * 2 + c)


PLANE = [(z, x, 0, 0) for z in range(4) for x in range(4) if z or x]
GROUP = [(0, 0, y, c) for y in range(4) for c in range(2) if y or c]
SIBLING = (0, 0, 0, 1)
STREAMS = 2
FAR = (2, 1, 3)
ORDERS = (
    (("x", "z", "y", 0, 1), ("z", "y", "x", 1, 2), ("y", "x", "z", 3, 1)),
    (("x", "z", "y", 0, 1), ("z", "y", "x", 1, 1), ("y", "x", "z", 2, 2)),
)


def order_tiles(dst_ref, src_ref, count, rows, meta):
    i32 = jnp.int32
    slots = dst_ref.shape[1]
    rows[...] = jnp.zeros_like(rows)
    rows[0:1, 0:slots] = dst_ref[...]
    rows[1:2, 0:slots] = src_ref[...]
    lane = lax.broadcasted_iota(i32, (128, 128), 1)
    sub = lax.broadcasted_iota(i32, (128, 128), 0)
    key = jnp.where(lane[0:1] < count, rows[0:1], jnp.where(lane[0:1] < slots, 16, 17))
    key_row = jnp.broadcast_to(key, (128, 128))
    key_col = jnp.transpose(key_row)
    src_col = jnp.transpose(jnp.broadcast_to(rows[1:2], (128, 128)))
    before = (key_row < key_col) | ((key_row == key_col) & (lane < sub))
    rank = jnp.sum(jnp.where(before, 1, 0), axis=1, keepdims=True)
    here = jnp.broadcast_to(rank, (128, 128)) == lane

    def down(value):
        return jnp.sum(value, axis=0, keepdims=True)

    perm = down(jnp.where(here, sub, 0))
    source = down(jnp.where(here, src_col, 0))
    sorted_key = down(jnp.where(here, key_col, 0))
    first = down(jnp.where(key_col < sorted_key, 1, 0))
    follows = jnp.where(lane[0:1] > first, 1, 0)
    upto = down(jnp.where(key_col <= lane, 1, 0))
    below = down(jnp.where(key_col < lane, 1, 0))
    some = jnp.where(upto > below, 1, 0)
    meta[0:1] = jnp.clip(perm, 0, slots - 1)
    meta[1:2] = jnp.clip(source, 0, 255)
    meta[2:3] = follows
    meta[3:4] = jnp.clip(upto - 1, 0, slots - 1)
    meta[4:5] = some


def split3(value):
    one = value.astype(jnp.bfloat16)
    rest = value - one.astype(jnp.float32)
    two = rest.astype(jnp.bfloat16)
    three = (rest - two.astype(jnp.float32)).astype(jnp.bfloat16)
    return one, two, three


def kernel(
    cnt_ref, dst_ref, src_ref, docs_ref, win_ref, wout_ref, dh_ref, tel_ref, tiles_any, out_ref,
    acc, lt, rows, meta, own_smem, sib_meta, sib_smem, raw_tiles, own_tiles, sib_tiles, lt_in, stage, stage_in,
    group_sum, group_in, mass_own, mass_in, mass_sum, mass_all, part, rs_in,
    tele, state, g00, g01, g10, g11, g20, g21, runs, final,
    loc_sem, sib_send, sib_recv, st_send, st_recv, gr_send, gr_recv,
    ms_send, ms_recv, mg_send, mg_recv, rs_send, rs_recv, ag_send, ag_recv,
):
    step = pl.program_id(0)
    h, d = lax.axis_index("hst"), lax.axis_index("doc")
    pos = {"z": h // 4, "x": lax.rem(h, 4), "y": d // 2}
    core = lax.rem(d, 2)
    y = pos["y"]
    topics = wout_ref.shape[0]
    mine = pl.multiple_of(core * 32, 32)
    other = pl.multiple_of(32 - core * 32, 32)

    def remote(src, dst, send, recv, to):
        return pltpu.make_async_remote_copy(
            src_ref=src, dst_ref=dst, send_sem=send, recv_sem=recv, device_id=peer(*to), device_id_type=MESH
        )

    def wait_bytes(ref, sem):
        pltpu.make_async_copy(ref, ref, sem).wait()

    own_copy = pltpu.make_async_copy(tiles_any, raw_tiles, loc_sem.at[0])
    meta_own = pltpu.make_async_copy(meta, own_smem, loc_sem.at[1])
    meta_local = pltpu.make_async_copy(sib_meta, sib_smem, loc_sem.at[2])
    meta_copy = remote(meta, sib_meta, sib_send.at[1], sib_recv.at[1], SIBLING)
    tile_copy = remote(own_tiles, sib_tiles, sib_send.at[2], sib_recv.at[2], SIBLING)
    stage_copies = [
        remote(stage.at[peer(*to)[0]], stage_in.at[j], st_send, st_recv, to)
        for j, to in enumerate(PLANE)
    ]
    group_copies = [
        remote(group_sum.at[peer(*to)[1] // 2], group_in.at[j], gr_send, gr_recv, to)
        for j, to in enumerate(GROUP)
    ]
    mass_copies = [
        remote(mass_own, mass_in.at[j], ms_send, ms_recv, to) for j, to in enumerate(PLANE)
    ]
    total_copies = [
        remote(mass_sum, mass_all.at[j], mg_send, mg_recv, to) for j, to in enumerate(GROUP)
    ]

    def flip_tiles():
        def flip(i, carry):
            for j in range(8):
                own_tiles[i * 8 + j] = jnp.transpose(raw_tiles[i * 8 + j])
            return carry

        lax.fori_loop(0, own_tiles.shape[0] // 8, flip, 0)

    @pl.when(step == 0)
    def _():
        barrier = pltpu.get_barrier_semaphore()
        for to in PLANE + GROUP:
            pl.semaphore_signal(barrier, inc=1, device_id=peer(*to), device_id_type=MESH)
        own_copy.start()
        acc[...] = jnp.zeros_like(acc)
        order_tiles(dst_ref, src_ref, cnt_ref[0], rows, meta)
        meta_own.start()

    @pl.when(step == 1)
    def _():
        own_copy.wait()
        flip_tiles()

    @pl.when(step == 2)
    def _():
        pl.semaphore_wait(pltpu.get_barrier_semaphore(), len(PLANE) + len(GROUP))
        meta_copy.start()
        tile_copy.start()
        slots = own_tiles.shape[0]
        colsum = jnp.sum(raw_tiles[...].astype(jnp.float32), axis=1)
        row = lax.broadcasted_iota(jnp.int32, (512, slots), 0)
        src = src_ref[...]
        used = lax.broadcasted_iota(jnp.int32, (1, slots), 1) < cnt_ref[0]
        spot = jnp.where(used, (src // 4) * 8 + src % 4, 7)
        onehot = jnp.where(row == spot, 1.0, 0.0).astype(jnp.bfloat16)
        degree = sum(jnp.dot(onehot, p, preferred_element_type=jnp.float32) for p in split3(colsum))
        stage[...] = degree.reshape(16, 4, 8, 128)
        for copy in stage_copies:
            copy.start()

    @pl.when(step == 4)
    def _():
        wait_bytes(stage_in, st_recv)
        total = stage[h]
        for j in range(len(PLANE)):
            total += stage_in[j]
        group_sum[...] = total
        for copy in group_copies:
            copy.start()
        wait_bytes(stage_in, st_send)
        meta_copy.wait()
        meta_local.start()

    owner = dh_ref[0]
    upper = jnp.where(owner >= 1024, 1.0, 0.0).astype(jnp.bfloat16)
    lower = jnp.where(owner >= 1024, 0.0, 1.0).astype(jnp.bfloat16)
    pts = []
    for c in range(0, docs_ref.shape[0], 1024):
        hidden = jax.nn.gelu(
            jnp.dot(docs_ref[c:c+1024], win_ref[...], preferred_element_type=jnp.float32), approximate=True
        ).astype(jnp.bfloat16)
        logits = lax.dot_general(wout_ref[...], hidden, NT, preferred_element_type=jnp.float32)
        weight = jnp.exp(logits - jnp.max(logits, axis=0, keepdims=True))
        probs = weight * (1.0 / jnp.sum(weight, axis=0, keepdims=True))
        high = probs.astype(jnp.bfloat16)
        low = (probs - high.astype(jnp.float32)).astype(jnp.bfloat16)
        both = jnp.concatenate([high, low], axis=0)
        pts.append(jnp.concatenate([both * lower[:, c:c+1024], both * upper[:, c:c+1024]], axis=0))
    pt = jnp.concatenate(pts, axis=1)
    spot = (owner & 1023)
    piece = 512
    for at in range(0, 1024, piece):
        row = lax.broadcasted_iota(jnp.int32, (piece, owner.shape[1]), 0)
        onehot = jnp.where(row == spot - at, 1.0, 0.0).astype(jnp.bfloat16)
        acc[at : at + piece] += lax.dot_general(onehot, pt, NT, preferred_element_type=jnp.float32)

    @pl.when(step == pl.num_programs(0) - 1)
    def _():
        mass = jnp.zeros((topics, 128), jnp.float32)
        for b in range(16):
            flat = jnp.transpose(acc[b % 8 * 128 : (b % 8 + 1) * 128, b // 8 * 128 : (b // 8 + 1) * 128])
            flat = flat[:topics] + flat[topics:]
            lt[b] = flat
            mass += flat * tel_ref[b : b + 1, :].astype(jnp.float32)
        lt_copy = remote(lt.at[:, pl.ds(other, 32), :], lt_in, sib_send.at[0], sib_recv.at[0], SIBLING)
        lt_copy.start()
        wide = jnp.concatenate([mass, jnp.zeros_like(mass)], axis=0)
        mass_own[...] = jnp.broadcast_to(jnp.sum(jnp.transpose(wide), axis=0, keepdims=True), (8, 128))
        for copy in mass_copies:
            copy.start()
        wait_bytes(group_in, gr_recv)
        total = group_sum[y]
        for j in range(len(GROUP)):
            total += group_in[j]
        inverse = (1.0 / jnp.maximum(total[0:4], 1.0))[:, None, :]

        def reduce_start(inst, s):
            copies = []
            for k in FAR:
                there = lax.rem(y + k, 4)
                copies.append(
                    remote(
                        part.at[s, pl.ds(there * 4, 4)], rs_in.at[inst, s, k - 1],
                        rs_send.at[inst, s], rs_recv.at[inst, s], (0, 0, k, 0),
                    )
                )
            for copy in copies:
                copy.start()

        def reduce_end(inst, s):
            wait_bytes(rs_in.at[inst, s], rs_recv.at[inst, s])
            total = part[s, pl.ds(y * 4, 4)] + rs_in[inst, s, 0] + rs_in[inst, s, 1] + rs_in[inst, s, 2]
            wait_bytes(rs_in.at[inst, s], rs_send.at[inst, s])
            return total

        lt_copy.wait_recv()
        for s in range(STREAMS):
            at = pl.multiple_of(core * 32 + s * 16, 16)
            part[s] = lt[:, pl.ds(at, 16), :] + lt_in[:, s * 16 : s * 16 + 16]
            reduce_start(0, s)

        wait_bytes(mass_in, ms_recv)
        total = mass_own[...]
        for j in range(len(PLANE)):
            total += mass_in[j]
        mass_sum[...] = total
        for copy in total_copies:
            copy.start()

        lt_copy.wait_send()
        wait_bytes(group_in, gr_send)
        wait_bytes(mass_in, ms_send)
        topic = [reduce_end(0, s) for s in range(STREAMS)]
        wait_bytes(mass_all, mg_recv)
        total = mass_sum[...]
        for j in range(len(GROUP)):
            total += mass_all[j]
        square = jnp.transpose(jnp.broadcast_to(total[0:1], (128, 128)))
        mass = jnp.where(core == 0, square[0:32], square[32:64])
        member = tel_ref[pl.ds(y * 4, 4), :].astype(jnp.float32)[:, None, :]
        for s in range(STREAMS):
            start = member * topic[s] / mass[None, s * 16 : s * 16 + 16]
            tele[s] = start
            state[s] = start
        wait_bytes(mass_all, mg_send)
        meta_own.wait()
        meta_local.wait()
        tile_copy.wait()

        def along(axis, k):
            return tuple(k if axis == name else 0 for name in "zxy") + (0,)

        class Stream:
            def __init__(self, hop, s, gathered):
                self.hop, self.s, self.gathered = hop, s, gathered

            def place(self, fixed, first, count):
                index = [fixed[axis] if axis in fixed else slice(None) for axis in "zxy"]
                return self.gathered.at[(*index, pl.ds(first, count))]

            def send(self, slot, axis, k, ref):
                at = (self.hop, self.s)
                copy = remote(ref, ref, ag_send.at[at], ag_recv.at[(*at, slot)], along(axis, k))
                copy.start()
                return copy

            def stage1(self):
                sent = (state[self.s] * inverse).astype(jnp.bfloat16)
                self.gathered[pos["z"], pos["x"], y] = sent
                for o, (a1, a2, a3, first, count) in enumerate(ORDERS[self.s]):
                    ref = self.place(pos, first, count)
                    for k in FAR:
                        self.send(o, a1, k, ref)

            def stage2(self):
                self.two, later = [], []
                for o, (a1, a2, a3, first, count) in enumerate(ORDERS[self.s]):
                    wait_bytes(self.gathered.at[0, 0, pl.ds(0, 3), pl.ds(0, count)], ag_recv.at[self.hop, self.s, o])
                    ref = self.place({a2: pos[a2], a3: pos[a3]}, first, count)
                    self.two.append({k: self.send(3 * o + 2 + k, a2, k, ref) for k in FAR})
                    later.append((a3, ref))
                for a3, ref in later:
                    for k in FAR:
                        self.send(12, a3, k, ref)

            def stage3(self):
                for k2 in (1, 3, 2):
                    for o, (a1, a2, a3, first, count) in enumerate(ORDERS[self.s]):
                        self.two[o][k2].wait_recv()
                        there = lax.rem(pos[a2] + 4 - k2, 4)
                        ref = self.place({a2: there, a3: pos[a3]}, first, count)
                        for k in FAR:
                            self.send(12, a3, k, ref)

            def multiply(self):
                wait_bytes(runs.at[:, pl.ds(0, 48)], ag_recv.at[self.hop, self.s, 12])
                lists = ((own_smem, own_tiles), (sib_smem, sib_tiles))
                batch = 64
                gathered, s = self.gathered, self.s

                def tile_body(i, run):
                    run = list(run)
                    for j in range(batch):
                        r = i * batch + j
                        for n, (m, t) in enumerate(lists):
                            b = m[1, r]
                            slab = gathered[b >> 6, (b >> 4) & 3, (b >> 2) & 3, b & 3]
                            prod = jnp.dot(slab, t[m[0, r]], preferred_element_type=jnp.float32)
                            run[n] = jnp.where(m[2, r] > 0, run[n], 0.0) + prod
                            runs[n, r] = run[n]
                    return tuple(run)

                zero = jnp.zeros((16, 128), jnp.float32)
                lax.fori_loop(0, own_tiles.shape[0] // batch, tile_body, (zero, zero))
                for blk in range(16):
                    value = zero
                    for n, (m, t) in enumerate(lists):
                        value += jnp.where(m[4, blk] > 0, runs[n, m[3, blk]], 0.0)
                    part[s, blk] = value
                reduce_start(self.hop + 1, s)

            def finish(self):
                inflow = reduce_end(self.hop + 1, self.s)
                state[self.s] = 0.85 * inflow + 0.15 * tele[self.s]

            def settle(self):
                wait_bytes(runs.at[:, pl.ds(0, 63)], ag_send.at[self.hop, self.s])

        streams = [[Stream(hop, s, g) for s, g in enumerate(gs)] for hop, gs in enumerate(((g00, g01), (g10, g11), (g20, g21)))]
        for one in streams[0]:
            one.stage1()
        for hop in range(HOPS):
            for one in streams[hop]:
                one.stage2()
            for one in streams[hop]:
                one.stage3()
            for one in streams[hop]:
                one.multiply()
            for s, one in enumerate(streams[hop]):
                one.finish()
                if hop + 1 < HOPS:
                    streams[hop + 1][s].stage1()
            for one in streams[hop]:
                one.settle()

        hosts_all = 128.0 * 256.0
        keep = pl.multiple_of(core * 2, 2)
        give = pl.multiple_of(2 - core * 2, 2)
        state[...] = hosts_all * state[...]
        last = remote(state.at[:, pl.ds(give, 2)], final.at[core], sib_send.at[3], sib_recv.at[3], SIBLING)
        last.start()
        final[core] = state[:, pl.ds(keep, 2)]
        last.wait()
        for j in range(2):
            out_ref[j * 128 : (j + 1) * 128, :] = jnp.transpose(final[:, :, j].reshape(64, 128))


def body(docs, w_in, w_out, doc_host, tiles, dst_block, src_block, tile_count, teleport):
    f32, bf16, i32 = jnp.float32, jnp.bfloat16, jnp.int32
    docs_dev, depth = docs.shape
    hidden, topics = w_out.shape
    slots = tiles.shape[0]
    steps = 8
    rows = docs_dev // steps

    def whole(*shape):
        return pl.BlockSpec(shape, lambda i: (0,) * len(shape))

    dma = pltpu.SemaphoreType.DMA
    return pl.pallas_call(
        kernel,
        grid=(steps,),
        out_shape=jax.ShapeDtypeStruct((256, topics), f32),
        in_specs=[
            pl.BlockSpec(memory_space=pltpu.SMEM),
            whole(1, slots),
            whole(1, slots),
            pl.BlockSpec((rows, depth), lambda i: (i, 0)),
            whole(depth, hidden),
            whole(topics, hidden),
            pl.BlockSpec((1, 1, rows), lambda i: (i, 0, 0)),
            whole(16, 128),
            pl.BlockSpec(memory_space=pl.ANY),
        ],
        out_specs=whole(256, topics),
        scratch_shapes=[
            pltpu.VMEM((1024, 256), f32),
            pltpu.VMEM((16, topics, 128), f32),
            pltpu.VMEM((8, 128), i32),
            pltpu.VMEM((8, 128), i32),
            pltpu.SMEM((8, 128), i32),
            pltpu.VMEM((8, 128), i32),
            pltpu.SMEM((8, 128), i32),
            pltpu.VMEM(tiles.shape, bf16),
            pltpu.VMEM(tiles.shape, bf16),
            pltpu.VMEM(tiles.shape, bf16),
            pltpu.VMEM((16, 32, 128), f32),
            pltpu.VMEM((16, 4, 8, 128), f32),
            pltpu.VMEM((15, 4, 8, 128), f32),
            pltpu.VMEM((4, 8, 128), f32),
            pltpu.VMEM((7, 8, 128), f32),
            pltpu.VMEM((8, 128), f32),
            pltpu.VMEM((15, 8, 128), f32),
            pltpu.VMEM((8, 128), f32),
            pltpu.VMEM((7, 8, 128), f32),
            pltpu.VMEM((STREAMS, 16, 16, 128), f32),
            pltpu.VMEM((HOPS + 1, STREAMS, 3, 4, 16, 128), f32),
            pltpu.VMEM((STREAMS, 4, 16, 128), f32),
            pltpu.VMEM((STREAMS, 4, 16, 128), f32),
            *[pltpu.VMEM((4, 4, 4, 4, 16, 128), bf16) for _ in range(HOPS * STREAMS)],
            pltpu.VMEM((2, slots, 16, 128), f32),
            pltpu.VMEM((2, STREAMS, 2, 16, 128), f32),
            dma((3,)), dma((4,)), dma((4,)), *[dma] * 8,
            dma((HOPS + 1, STREAMS)), dma((HOPS + 1, STREAMS)), dma((HOPS, STREAMS)), dma((HOPS, STREAMS, 13)),
        ],
        compiler_params=pltpu.CompilerParams(
            collective_id=0, has_side_effects=True, vmem_limit_bytes=58 << 20
        ),
        name="spread",
    )(
        tile_count, dst_block.reshape(1, slots), src_block.reshape(1, slots), docs, w_in, w_out.T,
        doc_host.reshape(steps, 1, rows), teleport.reshape(16, 128), tiles,
    )


def solution(mesh):
    placed = (
        P(("hst", "doc"), None),
        P(),
        P(),
        P(("hst", "doc")),
        P(("hst", "doc"), None, None),
        P(("hst", "doc")),
        P(("hst", "doc")),
        P(("hst", "doc")),
        P("hst"),
    )
    return jax.shard_map(
        body, mesh=mesh, in_specs=placed, out_specs=P(("hst", "doc"), None), check_vma=False
    )
```

```python
import jax
import jax.numpy as jnp
from jax import lax
from jax.experimental import pallas as pl
from jax.experimental.pallas import tpu as pltpu
from jax.sharding import PartitionSpec as P

HOPS = 3
MESH = pl.DeviceIdType.MESH
NT = (((1,), (1,)), ((), ()))


def peer(dz, dx, dy, dc):
    h, d = lax.axis_index("hst"), lax.axis_index("doc")
    z = lax.rem(h // 4 + dz, 4)
    x = lax.rem(lax.rem(h, 4) + dx, 4)
    y = lax.rem(d // 2 + dy, 4)
    c = lax.rem(lax.rem(d, 2) + dc, 2)
    return (z * 4 + x, y * 2 + c)


PLANE = [(z, x, 0, 0) for z in range(4) for x in range(4) if z or x]
GROUP = [(0, 0, y, c) for y in range(4) for c in range(2) if y or c]
SIBLING = (0, 0, 0, 1)
STREAMS = 2
FAR = (2, 1, 3)
ORDERS = (
    (("x", "z", "y", 0, 1), ("z", "y", "x", 1, 2), ("y", "x", "z", 3, 1)),
    (("x", "z", "y", 0, 1), ("z", "y", "x", 1, 1), ("y", "x", "z", 2, 2)),
)


def order_tiles(dst_ref, src_ref, count, rows, meta):
    i32 = jnp.int32
    slots = dst_ref.shape[1]
    rows[...] = jnp.zeros_like(rows)
    rows[0:1, 0:slots] = dst_ref[...]
    rows[1:2, 0:slots] = src_ref[...]
    lane = lax.broadcasted_iota(i32, (128, 128), 1)
    sub = lax.broadcasted_iota(i32, (128, 128), 0)
    key = jnp.where(lane[0:1] < count, rows[0:1], jnp.where(lane[0:1] < slots, 16, 17))
    key_row = jnp.broadcast_to(key, (128, 128))
    key_col = jnp.transpose(key_row)
    src_col = jnp.transpose(jnp.broadcast_to(rows[1:2], (128, 128)))
    before = (key_row < key_col) | ((key_row == key_col) & (lane < sub))
    rank = jnp.sum(jnp.where(before, 1, 0), axis=1, keepdims=True)
    here = jnp.broadcast_to(rank, (128, 128)) == lane

    def down(value):
        return jnp.sum(value, axis=0, keepdims=True)

    perm = down(jnp.where(here, sub, 0))
    source = down(jnp.where(here, src_col, 0))
    sorted_key = down(jnp.where(here, key_col, 0))
    first = down(jnp.where(key_col < sorted_key, 1, 0))
    follows = jnp.where(lane[0:1] > first, 1, 0)
    upto = down(jnp.where(key_col <= lane, 1, 0))
    below = down(jnp.where(key_col < lane, 1, 0))
    some = jnp.where(upto > below, 1, 0)
    meta[0:1] = jnp.clip(perm, 0, slots - 1)
    meta[1:2] = jnp.clip(source, 0, 255)
    meta[2:3] = follows
    meta[3:4] = jnp.clip(upto - 1, 0, slots - 1)
    meta[4:5] = some


def split3(value):
    one = value.astype(jnp.bfloat16)
    rest = value - one.astype(jnp.float32)
    two = rest.astype(jnp.bfloat16)
    three = (rest - two.astype(jnp.float32)).astype(jnp.bfloat16)
    return one, two, three


def kernel(
    cnt_ref, dst_ref, src_ref, docs_ref, win_ref, wout_ref, dh_ref, tel_ref, tiles_ref, tiles_any, out_ref,
    acc, lt, rows, meta, own_smem, sib_meta, sib_smem, raw_tiles, own_tiles, sib_tiles, lt_in, stage, stage_in,
    group_sum, group_in, mass_own, mass_in, mass_sum, mass_all, part, rs_in,
    tele, state, g00, g01, g10, g11, g20, g21, runs, final,
    loc_sem, sib_send, sib_recv, st_send, st_recv, gr_send, gr_recv,
    ms_send, ms_recv, mg_send, mg_recv, rs_send, rs_recv, ag_send, ag_recv,
):
    step = pl.program_id(0)
    h, d = lax.axis_index("hst"), lax.axis_index("doc")
    pos = {"z": h // 4, "x": lax.rem(h, 4), "y": d // 2}
    core = lax.rem(d, 2)
    y = pos["y"]
    topics = wout_ref.shape[0]
    mine = pl.multiple_of(core * 32, 32)
    other = pl.multiple_of(32 - core * 32, 32)

    def remote(src, dst, send, recv, to):
        return pltpu.make_async_remote_copy(
            src_ref=src, dst_ref=dst, send_sem=send, recv_sem=recv, device_id=peer(*to), device_id_type=MESH
        )

    def wait_bytes(ref, sem):
        pltpu.make_async_copy(ref, ref, sem).wait()

    own_copy = pltpu.make_async_copy(tiles_any, raw_tiles, loc_sem.at[0])
    meta_own = pltpu.make_async_copy(meta, own_smem, loc_sem.at[1])
    meta_local = pltpu.make_async_copy(sib_meta, sib_smem, loc_sem.at[2])
    meta_copy = remote(meta, sib_meta, sib_send.at[1], sib_recv.at[1], SIBLING)
    tile_copy = remote(own_tiles, sib_tiles, sib_send.at[2], sib_recv.at[2], SIBLING)
    stage_copies = [
        remote(stage.at[peer(*to)[0]], stage_in.at[j], st_send, st_recv, to)
        for j, to in enumerate(PLANE)
    ]
    group_copies = [
        remote(group_sum.at[peer(*to)[1] // 2], group_in.at[j], gr_send, gr_recv, to)
        for j, to in enumerate(GROUP)
    ]
    mass_copies = [
        remote(mass_own, mass_in.at[j], ms_send, ms_recv, to) for j, to in enumerate(PLANE)
    ]
    total_copies = [
        remote(mass_sum, mass_all.at[j], mg_send, mg_recv, to) for j, to in enumerate(GROUP)
    ]

    @pl.when(step == 0)
    def _():
        barrier = pltpu.get_barrier_semaphore()
        for to in PLANE + GROUP:
            pl.semaphore_signal(barrier, inc=1, device_id=peer(*to), device_id_type=MESH)
        own_copy.start()
        acc[...] = jnp.zeros_like(acc)
        order_tiles(dst_ref, src_ref, cnt_ref[0], rows, meta)
        meta_own.start()

    @pl.when(step == 2)
    def _():
        pl.semaphore_wait(pltpu.get_barrier_semaphore(), len(PLANE) + len(GROUP))
        meta_copy.start()
        own_copy.wait()
        slots = raw_tiles.shape[0]
        colsum = jnp.sum(raw_tiles[...].astype(jnp.float32), axis=1)
        row = lax.broadcasted_iota(jnp.int32, (512, slots), 0)
        src = src_ref[...]
        used = lax.broadcasted_iota(jnp.int32, (1, slots), 1) < cnt_ref[0]
        spot = jnp.where(used, (src // 4) * 8 + src % 4, 7)
        onehot = jnp.where(row == spot, 1.0, 0.0).astype(jnp.bfloat16)
        degree = sum(jnp.dot(onehot, p, preferred_element_type=jnp.float32) for p in split3(colsum))
        stage[...] = degree.reshape(16, 4, 8, 128)
        for copy in stage_copies:
            copy.start()

    @pl.when(step == 4)
    def _():
        wait_bytes(stage_in, st_recv)
        total = stage[h]
        for j in range(len(PLANE)):
            total += stage_in[j]
        group_sum[...] = total
        for copy in group_copies:
            copy.start()
        wait_bytes(stage_in, st_send)
        meta_copy.wait()
        meta_local.start()

    owner = dh_ref[0]
    upper = jnp.where(owner >= 1024, 1.0, 0.0).astype(jnp.bfloat16)
    lower = jnp.where(owner >= 1024, 0.0, 1.0).astype(jnp.bfloat16)
    pts = []
    for c in range(0, docs_ref.shape[0], 1024):
        hidden = jax.nn.gelu(
            jnp.dot(docs_ref[c:c+1024], win_ref[...], preferred_element_type=jnp.float32), approximate=True
        ).astype(jnp.bfloat16)
        logits = lax.dot_general(wout_ref[...], hidden, NT, preferred_element_type=jnp.float32)
        weight = jnp.exp(logits - jnp.max(logits, axis=0, keepdims=True))
        probs = weight * (1.0 / jnp.sum(weight, axis=0, keepdims=True))
        high = probs.astype(jnp.bfloat16)
        low = (probs - high.astype(jnp.float32)).astype(jnp.bfloat16)
        both = jnp.concatenate([high, low], axis=0)
        pts.append(jnp.concatenate([both * lower[:, c:c+1024], both * upper[:, c:c+1024]], axis=0))
    pt = jnp.concatenate(pts, axis=1)
    for j in range(tiles_ref.shape[0]):
        own_tiles[step * tiles_ref.shape[0] + j] = jnp.transpose(tiles_ref[j])
    spot = (owner & 1023)
    piece = 512
    for at in range(0, 1024, piece):
        row = lax.broadcasted_iota(jnp.int32, (piece, owner.shape[1]), 0)
        onehot = jnp.where(row == spot - at, 1.0, 0.0).astype(jnp.bfloat16)
        acc[at : at + piece] += lax.dot_general(onehot, pt, NT, preferred_element_type=jnp.float32)

    @pl.when(step == pl.num_programs(0) - 1)
    def _():
        mass = jnp.zeros((topics, 128), jnp.float32)
        for b in range(16):
            flat = jnp.transpose(acc[b % 8 * 128 : (b % 8 + 1) * 128, b // 8 * 128 : (b // 8 + 1) * 128])
            flat = flat[:topics] + flat[topics:]
            lt[b] = flat
            mass += flat * tel_ref[b : b + 1, :].astype(jnp.float32)
        lt_copy = remote(lt.at[:, pl.ds(other, 32), :], lt_in, sib_send.at[0], sib_recv.at[0], SIBLING)
        lt_copy.start()
        wide = jnp.concatenate([mass, jnp.zeros_like(mass)], axis=0)
        mass_own[...] = jnp.broadcast_to(jnp.sum(jnp.transpose(wide), axis=0, keepdims=True), (8, 128))
        for copy in mass_copies:
            copy.start()
        tile_copy.start()
        wait_bytes(group_in, gr_recv)
        total = group_sum[y]
        for j in range(len(GROUP)):
            total += group_in[j]
        inverse = (1.0 / jnp.maximum(total[0:4], 1.0))[:, None, :]

        def reduce_start(inst, s):
            copies = []
            for k in FAR:
                there = lax.rem(y + k, 4)
                copies.append(
                    remote(
                        part.at[s, pl.ds(there * 4, 4)], rs_in.at[inst, s, k - 1],
                        rs_send.at[inst, s], rs_recv.at[inst, s], (0, 0, k, 0),
                    )
                )
            for copy in copies:
                copy.start()

        def reduce_end(inst, s):
            wait_bytes(rs_in.at[inst, s], rs_recv.at[inst, s])
            total = part[s, pl.ds(y * 4, 4)] + rs_in[inst, s, 0] + rs_in[inst, s, 1] + rs_in[inst, s, 2]
            wait_bytes(rs_in.at[inst, s], rs_send.at[inst, s])
            return total

        lt_copy.wait_recv()
        for s in range(STREAMS):
            at = pl.multiple_of(core * 32 + s * 16, 16)
            part[s] = lt[:, pl.ds(at, 16), :] + lt_in[:, s * 16 : s * 16 + 16]
            reduce_start(0, s)

        wait_bytes(mass_in, ms_recv)
        total = mass_own[...]
        for j in range(len(PLANE)):
            total += mass_in[j]
        mass_sum[...] = total
        for copy in total_copies:
            copy.start()

        lt_copy.wait_send()
        wait_bytes(group_in, gr_send)
        wait_bytes(mass_in, ms_send)
        topic = [reduce_end(0, s) for s in range(STREAMS)]
        wait_bytes(mass_all, mg_recv)
        total = mass_sum[...]
        for j in range(len(GROUP)):
            total += mass_all[j]
        square = jnp.transpose(jnp.broadcast_to(total[0:1], (128, 128)))
        mass = jnp.where(core == 0, square[0:32], square[32:64])
        member = tel_ref[pl.ds(y * 4, 4), :].astype(jnp.float32)[:, None, :]
        for s in range(STREAMS):
            start = member * topic[s] / mass[None, s * 16 : s * 16 + 16]
            tele[s] = start
            state[s] = start
        wait_bytes(mass_all, mg_send)
        meta_own.wait()
        meta_local.wait()
        tile_copy.wait()

        def along(axis, k):
            return tuple(k if axis == name else 0 for name in "zxy") + (0,)

        class Stream:
            def __init__(self, hop, s, gathered):
                self.hop, self.s, self.gathered = hop, s, gathered

            def place(self, fixed, first, count):
                index = [fixed[axis] if axis in fixed else slice(None) for axis in "zxy"]
                return self.gathered.at[(*index, pl.ds(first, count))]

            def send(self, slot, axis, k, ref):
                at = (self.hop, self.s)
                copy = remote(ref, ref, ag_send.at[at], ag_recv.at[(*at, slot)], along(axis, k))
                copy.start()
                return copy

            def stage1(self):
                sent = (state[self.s] * inverse).astype(jnp.bfloat16)
                self.gathered[pos["z"], pos["x"], y] = sent
                for o, (a1, a2, a3, first, count) in enumerate(ORDERS[self.s]):
                    ref = self.place(pos, first, count)
                    for k in FAR:
                        self.send(o, a1, k, ref)

            def stage2(self):
                self.two, later = [], []
                for o, (a1, a2, a3, first, count) in enumerate(ORDERS[self.s]):
                    wait_bytes(self.gathered.at[0, 0, pl.ds(0, 3), pl.ds(0, count)], ag_recv.at[self.hop, self.s, o])
                    ref = self.place({a2: pos[a2], a3: pos[a3]}, first, count)
                    self.two.append({k: self.send(3 * o + 2 + k, a2, k, ref) for k in FAR})
                    later.append((a3, ref))
                for a3, ref in later:
                    for k in FAR:
                        self.send(12, a3, k, ref)

            def stage3(self):
                for k2 in (1, 3, 2):
                    for o, (a1, a2, a3, first, count) in enumerate(ORDERS[self.s]):
                        self.two[o][k2].wait_recv()
                        there = lax.rem(pos[a2] + 4 - k2, 4)
                        ref = self.place({a2: there, a3: pos[a3]}, first, count)
                        for k in FAR:
                            self.send(12, a3, k, ref)

            def multiply(self):
                wait_bytes(runs.at[:, pl.ds(0, 48)], ag_recv.at[self.hop, self.s, 12])
                lists = ((own_smem, own_tiles), (sib_smem, sib_tiles))
                batch = 64
                gathered, s = self.gathered, self.s

                def tile_body(i, run):
                    run = list(run)
                    for j in range(batch):
                        r = i * batch + j
                        for n, (m, t) in enumerate(lists):
                            b = m[1, r]
                            slab = gathered[b >> 6, (b >> 4) & 3, (b >> 2) & 3, b & 3]
                            prod = jnp.dot(slab, t[m[0, r]], preferred_element_type=jnp.float32)
                            run[n] = jnp.where(m[2, r] > 0, run[n], 0.0) + prod
                            runs[n, r] = run[n]
                    return tuple(run)

                zero = jnp.zeros((16, 128), jnp.float32)
                lax.fori_loop(0, own_tiles.shape[0] // batch, tile_body, (zero, zero))
                for blk in range(16):
                    value = zero
                    for n, (m, t) in enumerate(lists):
                        value += jnp.where(m[4, blk] > 0, runs[n, m[3, blk]], 0.0)
                    part[s, blk] = value
                reduce_start(self.hop + 1, s)

            def finish(self):
                inflow = reduce_end(self.hop + 1, self.s)
                state[self.s] = 0.85 * inflow + 0.15 * tele[self.s]

            def settle(self):
                wait_bytes(runs.at[:, pl.ds(0, 63)], ag_send.at[self.hop, self.s])

        streams = [[Stream(hop, s, g) for s, g in enumerate(gs)] for hop, gs in enumerate(((g00, g01), (g10, g11), (g20, g21)))]
        for one in streams[0]:
            one.stage1()
        for hop in range(HOPS):
            for one in streams[hop]:
                one.stage2()
            for one in streams[hop]:
                one.stage3()
            for one in streams[hop]:
                one.multiply()
            for s, one in enumerate(streams[hop]):
                one.finish()
                if hop + 1 < HOPS:
                    streams[hop + 1][s].stage1()
            for one in streams[hop]:
                one.settle()

        hosts_all = 128.0 * 256.0
        keep = pl.multiple_of(core * 2, 2)
        give = pl.multiple_of(2 - core * 2, 2)
        state[...] = hosts_all * state[...]
        last = remote(state.at[:, pl.ds(give, 2)], final.at[core], sib_send.at[3], sib_recv.at[3], SIBLING)
        last.start()
        final[core] = state[:, pl.ds(keep, 2)]
        last.wait()
        for j in range(2):
            out_ref[j * 128 : (j + 1) * 128, :] = jnp.transpose(final[:, :, j].reshape(64, 128))


def body(docs, w_in, w_out, doc_host, tiles, dst_block, src_block, tile_count, teleport):
    f32, bf16, i32 = jnp.float32, jnp.bfloat16, jnp.int32
    docs_dev, depth = docs.shape
    hidden, topics = w_out.shape
    slots = tiles.shape[0]
    steps = 8
    rows = docs_dev // steps

    def whole(*shape):
        return pl.BlockSpec(shape, lambda i: (0,) * len(shape))

    dma = pltpu.SemaphoreType.DMA
    return pl.pallas_call(
        kernel,
        grid=(steps,),
        out_shape=jax.ShapeDtypeStruct((256, topics), f32),
        in_specs=[
            pl.BlockSpec(memory_space=pltpu.SMEM),
            whole(1, slots),
            whole(1, slots),
            pl.BlockSpec((rows, depth), lambda i: (i, 0)),
            whole(depth, hidden),
            whole(topics, hidden),
            pl.BlockSpec((1, 1, rows), lambda i: (i, 0, 0)),
            whole(16, 128),
            pl.BlockSpec((slots // steps, 128, 128), lambda i: (i, 0, 0)),
            pl.BlockSpec(memory_space=pl.ANY),
        ],
        out_specs=whole(256, topics),
        scratch_shapes=[
            pltpu.VMEM((1024, 256), f32),
            pltpu.VMEM((16, topics, 128), f32),
            pltpu.VMEM((8, 128), i32),
            pltpu.VMEM((8, 128), i32),
            pltpu.SMEM((8, 128), i32),
            pltpu.VMEM((8, 128), i32),
            pltpu.SMEM((8, 128), i32),
            pltpu.VMEM(tiles.shape, bf16),
            pltpu.VMEM(tiles.shape, bf16),
            pltpu.VMEM(tiles.shape, bf16),
            pltpu.VMEM((16, 32, 128), f32),
            pltpu.VMEM((16, 4, 8, 128), f32),
            pltpu.VMEM((15, 4, 8, 128), f32),
            pltpu.VMEM((4, 8, 128), f32),
            pltpu.VMEM((7, 8, 128), f32),
            pltpu.VMEM((8, 128), f32),
            pltpu.VMEM((15, 8, 128), f32),
            pltpu.VMEM((8, 128), f32),
            pltpu.VMEM((7, 8, 128), f32),
            pltpu.VMEM((STREAMS, 16, 16, 128), f32),
            pltpu.VMEM((HOPS + 1, STREAMS, 3, 4, 16, 128), f32),
            pltpu.VMEM((STREAMS, 4, 16, 128), f32),
            pltpu.VMEM((STREAMS, 4, 16, 128), f32),
            *[pltpu.VMEM((4, 4, 4, 4, 16, 128), bf16) for _ in range(HOPS * STREAMS)],
            pltpu.VMEM((2, slots, 16, 128), f32),
            pltpu.VMEM((2, STREAMS, 2, 16, 128), f32),
            dma((3,)), dma((4,)), dma((4,)), *[dma] * 8,
            dma((HOPS + 1, STREAMS)), dma((HOPS + 1, STREAMS)), dma((HOPS, STREAMS)), dma((HOPS, STREAMS, 13)),
        ],
        compiler_params=pltpu.CompilerParams(
            collective_id=0, has_side_effects=True, vmem_limit_bytes=58 << 20
        ),
        name="spread",
    )(
        tile_count, dst_block.reshape(1, slots), src_block.reshape(1, slots), docs, w_in, w_out.T,
        doc_host.reshape(steps, 1, rows), teleport.reshape(16, 128), tiles, tiles,
    )


def solution(mesh):
    placed = (
        P(("hst", "doc"), None),
        P(),
        P(),
        P(("hst", "doc")),
        P(("hst", "doc"), None, None),
        P(("hst", "doc")),
        P(("hst", "doc")),
        P(("hst", "doc")),
        P("hst"),
    )
    return jax.shard_map(
        body, mesh=mesh, in_specs=placed, out_specs=P(("hst", "doc"), None), check_vma=False
    )
```
